32 devices in a mesh: seq: 4 (over x, core), batch: 2 (over y), mp: 4 (over z).
Axes of the slice: x: 2, y: 2, z: 4, core: 2. Of those that a mesh axis runs over, the one named last changes fastest.
Arguments:
- xs: bfloat16 [2, 1536, 8192], P('batch', 'seq', 'mp'), may hold values from -6 to 6
- gate_z: bfloat16 [2, 1536, 8192], P('batch', 'seq', 'mp'), may hold values from -16 to 16
- b_in: bfloat16 [2, 1536, 128], P('batch', 'seq'), may hold values from -1.796875 to 1.796875
- c_in: bfloat16 [2, 1536, 128], P('batch', 'seq'), may hold values from -1.796875 to 1.796875
- log_decay: float32 [2, 1536, 128], P('batch', 'seq', 'mp'), may hold values from -4 to 0
- d_skip: float32 [128], P('mp'), may hold values from 0.5 to 2
- norm_gain: float32 [8192], P('mp'), may hold values from 0.5 to 1.5
- queries: bfloat16 [2, 1536, 4096], P('batch', 'seq', 'mp'), may hold values from -6 to 6
- keys_new: bfloat16 [2, 1536, 1024], P('batch', 'seq', 'mp'), may hold values from -6 to 6
- values_new: bfloat16 [2, 1536, 1024], P('batch', 'seq', 'mp'), may hold values from -6 to 6
- kv_pool: bfloat16 [64, 2, 64, 1024], P('batch', None, None, 'mp'), may hold values from -6 to 6
- state_pool: bfloat16 [128, 128, 16, 128], P('batch', 'mp'), may hold values from -6 to 6
- new_len: int32 [2], P('batch'), may hold values from 384 to 1536, as said below
- cached_blocks: int32 [2], P('batch'), may hold values from 1 to 4, 6 in all
- kv_owner: int32 [2, 4, 1], P('batch'), may hold values from 0 to 1; in each aligned block of 4 rows (0 to 3, 4 to 7, ..., all dimensions but the last counted through in order) at most 3 rows name the same one
- kv_slot: int32 [2, 4], P('batch'), may hold values from 0 to 31
- state_owner: int32 [2, 4, 1], P('batch'), may hold values from 0 to 1; in each aligned block of 4 rows (0 to 3, 4 to 7, ..., all dimensions but the last counted through in order) at most 3 rows name the same one
- state_slot: int32 [2, 4], P('batch'), may hold values from 0 to 63
Outputs:
- ssm_out: bfloat16 [2, 1536, 8192], P('batch', 'seq', 'mp')
- attn_out: bfloat16 [2, 1536, 4096], P('batch', 'seq', 'mp')
The draws below stay inside these ranges and needn't reach their ends.
Inputs may be any that keep to these rules, and one draw needn't show every extreme that they name: `new_len`: at least 384; some prompt has exactly 1536. `kv_owner`: among the 4 entries of one prompt's list no owner appears more than 3 times. `state_owner`: among the 4 pieces of one prompt no owner appears more than 3 times.
All inputs are finite; a program needn't handle non-finite values. No bound on the sum of `cached_blocks` on one device may be relied on, other than what follows from the above.
Results may differ from the reference program's by a relative error of at most 0.0085.
Values may be sent and summed in bfloat16 or wider, within the bound.
No kernel may reach another device: no remote copies, remote signals or barrier semaphores. Data moves between devices by JAX's collectives and lax.ppermute only.
A program may use at most 128 MiB of HBM per device.

```python
import math
import jax
import jax.numpy as jnp
import numpy as np
from jax import lax

STRETCH = 384
H = 128
P_SIZE = 64
N = 128
QH = 32
KVH = 8
HD = 128
BQ = 128
BLK = 64
POOL_DEV = 32
SPOOL_DEV = 64
PROMPT_COUNT = 2
NEW_TOKEN_SLOTS = 1536
MAXB = 4
CAP = 3
SPIECES = 4
PP = 16
POOL_ALL = 64
SPOOL_ALL = 128
N_BATCH = 2


def draw_new_len(key, part):
    first_key, second_key = jax.random.split(jax.random.fold_in(key, 3))
    extra = jax.random.randint(first_key, (PROMPT_COUNT,), 0, 3 * STRETCH + 1)
    longest = jax.random.randint(second_key, (), 0, PROMPT_COUNT)
    lengths_all = STRETCH + extra
    return jnp.where(jnp.arange(PROMPT_COUNT) == longest, NEW_TOKEN_SLOTS, lengths_all).astype(jnp.int32)


def draw_log_decay(key, part):
    every_key_row = jax.random.split(jax.random.fold_in(key, 5), 7)
    slow_share = 0.5
    slow_heads = jax.random.uniform(every_key_row[0], (H,)) < slow_share
    slow_rate = jnp.exp(jax.random.uniform(every_key_row[1], (H,), minval=math.log(1.0 / (8.0 * NEW_TOKEN_SLOTS)), maxval=math.log(1.0 / (3.0 * NEW_TOKEN_SLOTS))))
    quick_rate = jnp.exp(jax.random.uniform(every_key_row[2], (H,), minval=math.log(1.0 / 400.0), maxval=math.log(1.0 / 30.0)))
    rates = jnp.where(slow_heads, slow_rate, quick_rate)
    per_prompt = jnp.exp(jax.random.uniform(every_key_row[3], (PROMPT_COUNT, 1, 1), minval=math.log(0.5), maxval=math.log(2.0)))
    jitter = jnp.exp(jax.random.uniform(every_key_row[4], (PROMPT_COUNT, NEW_TOKEN_SLOTS, H), minval=math.log(0.5), maxval=math.log(2.0)))
    token_runs = jax.random.randint(every_key_row[5], (PROMPT_COUNT, 3), 0, NEW_TOKEN_SLOTS)
    masked_out_flags = jnp.any(jnp.arange(NEW_TOKEN_SLOTS)[None, :, None] == token_runs[:, None, :], axis=-1)
    losses = jax.random.uniform(every_key_row[6], (PROMPT_COUNT, NEW_TOKEN_SLOTS, H), minval=math.log(0.5), maxval=math.log(0.8))
    values_all = -rates[None, None, :] * per_prompt * jitter + jnp.where(masked_out_flags[:, :, None], losses, 0.0)
    return jnp.clip(values_all, -4.0, 0.0).astype(jnp.float32)


def draw_gate_z(key, part):
    first_key, second_key, third_key = jax.random.split(jax.random.fold_in(key, 11), 3)
    channels = H * P_SIZE
    ramp = jnp.exp(math.log(3.0) * jnp.arange(channels, dtype=jnp.float32) / channels)
    column_scale = jnp.exp(jax.random.uniform(first_key, (channels,), minval=0.0, maxval=math.log(4.0)))
    row_scale = jnp.exp(jax.random.uniform(second_key, (PROMPT_COUNT, NEW_TOKEN_SLOTS, 1), minval=0.0, maxval=math.log(10.0)))
    base = jax.random.normal(third_key, (PROMPT_COUNT, NEW_TOKEN_SLOTS, channels))
    return jnp.clip(0.15 * base * ramp * column_scale * row_scale, -16.0, 16.0).astype(jnp.bfloat16)


def drawn_pair(key):
    base_key = jax.random.fold_in(key, 17)
    query_key, fresh_key = jax.random.split(base_key, 2)
    group = QH // KVH
    query_all = jax.random.normal(query_key, (PROMPT_COUNT, NEW_TOKEN_SLOTS, KVH, group, HD))
    fresh_all = jax.random.normal(fresh_key, (PROMPT_COUNT, NEW_TOKEN_SLOTS, KVH, HD))
    query_all = jnp.clip(query_all, -6.0, 6.0).reshape(PROMPT_COUNT, NEW_TOKEN_SLOTS, QH * HD)
    fresh_all = jnp.clip(fresh_all, -6.0, 6.0).reshape(PROMPT_COUNT, NEW_TOKEN_SLOTS, KVH * HD)
    return (query_all, fresh_all)


def draw_queries(key, part):
    return drawn_pair(key)[0].astype(jnp.bfloat16)


def draw_keys_new(key, part):
    return drawn_pair(key)[1].astype(jnp.bfloat16)


def set_ends(values, stream_key, smallest, largest):
    longest = values.shape.index(max(values.shape))
    spots = []
    for shift in (0, 1):
        where = [jax.random.randint(jax.random.fold_in(stream_key, axis), (), 0, length) for axis, length in enumerate(values.shape)]
        where[longest] = (where[longest] + shift) % values.shape[longest]
        spots.append(tuple(where))
    return values.at[spots[0]].set(smallest).at[spots[1]].set(largest)


def shard_levels(key, extent, shards, smallest, high):
    gain = 1.0
    for dim, blocks in shards:
        heights = jax.random.uniform(jax.random.fold_in(jax.random.fold_in(key, 6), dim), (blocks,), jnp.float32, smallest / len(shards), high / len(shards))
        gain = gain * jnp.repeat(jnp.exp(heights), extent[dim] // blocks).reshape((-1,) + (1,) * (len(extent) - 1 - dim))
    return gain


def profile(amount, total, limit, lean):
    weights = [(1 << 20) // math.isqrt(standing ** lean) + 1 for standing in range(2, amount + 1)]
    rest, holding = total - limit - (amount - 1), [1] * (amount - 1)
    while rest > 0:
        movable = [i for i in range(amount - 1) if holding[i] < limit]
        pool, left = sum([weights[i] for i in movable]), rest
        for i in movable:
            more = min(limit - holding[i], max(1, left * weights[i] // pool), rest)
            holding[i] = holding[i] + more
            rest = rest - more
    return np.array([limit] + holding)


def ragged(stream_key, amount, total, limit, slope):
    if amount == 2:
        one = jax.random.randint(stream_key, (), max(1, total - limit), min(limit, total - 1) + 1)
        return jnp.stack([one, total - one])
    sizes = jnp.asarray(profile(amount, total, limit, slope), jnp.int32)
    pairs = (amount - 1) // 2
    source_of, taker = sizes[1:1 + 2 * pairs:2], sizes[2:2 + 2 * pairs:2]
    room = jnp.minimum(source_of - 1, limit - taker)
    moved = jax.random.randint(jax.random.fold_in(stream_key, 1), (pairs,), 0, 1 << 20) % (room + 1)
    sizes = sizes.at[1:1 + 2 * pairs:2].set(source_of - moved).at[2:2 + 2 * pairs:2].set(taker + moved)
    return sizes[jax.random.permutation(jax.random.fold_in(stream_key, 2), amount)]


def routed_block(own_key, own, number, rows, count, top, bound, slope):
    sequence = jax.random.permutation(own_key, count)
    packed, ordinary = shares(count, rows * top, bound, slope, True), shares(count, rows * top, bound, slope, False)
    places = jnp.arange(count)

    def named(tallies, rotation):
        used = int((tallies > 0).sum())
        fixed = max(1, used // 4)
        moved = fixed + (places - fixed + rotation * (used - fixed)) % max(1, count - fixed)
        return jnp.zeros((count,), jnp.int32).at[sequence[jnp.where(places < fixed, places, moved)]].set(jnp.asarray(tallies, jnp.int32))

    tallies = jnp.where(number % 4 == 0, named(packed, number // 4), named(ordinary, number - number // 4 - 1))
    mixed = jax.random.permutation(jax.random.fold_in(own, 3), count)
    donor, taker = mixed[0:count // 2 * 2:2], mixed[1:count // 2 * 2:2]
    room = jnp.minimum(tallies[donor] - 1, bound - tallies[taker]) // 2
    room = jnp.where((donor == sequence[0]) | (taker == sequence[0]) | (tallies[taker] == 0), 0, jnp.maximum(room, 0))
    moved = jax.random.randint(jax.random.fold_in(own, 4), (count // 2,), 0, 1 << 20) % (room + 1)
    tallies = tallies.at[donor].add(-moved).at[taker].add(moved)
    members = jnp.searchsorted(jnp.cumsum(tallies), jnp.arange(rows * top), side="right").astype(jnp.int32)
    table = members.reshape(top, rows).T
    table = table[jax.random.permutation(jax.random.fold_in(own, 1), rows)]
    rotation = jax.random.randint(jax.random.fold_in(own, 2), (rows, 1), 0, top)
    return jnp.take_along_axis(table, (jnp.arange(top)[None, :] + rotation) % top, axis=1)


def shares(amount, total, bound, lean, full):
    portions = [(1 << 20) // math.isqrt(rank ** lean) + 1 for rank in range(1, amount + 1)]
    largest = bound if full else min(bound, max(-(-total // amount), total * portions[0] // sum(portions)))
    least = 1 if total - largest >= amount - 1 else 0
    counts, rest = [largest] + [least] * (amount - 1), total - largest - least * (amount - 1)
    while rest > 0:
        movable = [i for i in range(1, amount) if counts[i] < largest] or [i for i in range(1, amount) if counts[i] < bound]
        pool, left = sum([portions[i] for i in movable]), rest
        for i in movable:
            more = min(bound - counts[i], max(1, left * portions[i] // pool), rest)
            counts[i] = counts[i] + more
            rest = rest - more
    return np.array(counts)


def noise(rng, extent, deviation, reach, shards=(), kind=jnp.bfloat16):
    array = jax.random.normal(rng, extent, jnp.float32) * deviation
    if len(shards) > 0:
        array = shard_levels(rng, extent, shards, -0.22, 0.18) * array
    return jnp.clip(array, min=-reach, max=reach).astype(kind)


def setup_inputs(seed: int = 0) -> dict:
    seeds = jax.random.split(jax.random.key(seed), 19)
    xs = noise(seeds[0], (PROMPT_COUNT, NEW_TOKEN_SLOTS, H * P_SIZE), 1.0, 6.0, ((0, 2), (1, 4), (2, 4)))
    gate_z = draw_gate_z(jax.random.fold_in(seeds[18], 71), 0)
    b_in = noise(seeds[2], (PROMPT_COUNT, NEW_TOKEN_SLOTS, N), 0.3, 1.796875, ((0, 2), (1, 4)))
    c_in = noise(seeds[3], (PROMPT_COUNT, NEW_TOKEN_SLOTS, N), 0.3, 1.796875, ((0, 2), (1, 4)))
    log_decay = draw_log_decay(jax.random.fold_in(seeds[18], 71), 0)
    d_skip = jnp.clip(jnp.exp(math.log(2.0) - 1.3862944 * jax.random.uniform(seeds[5], (H,), jnp.float32) ** shard_levels(seeds[5], (H,), ((0, 4),), -0.2, 0.2)), 0.5, 2.0)
    norm_gain = jnp.clip(1.0 + 0.1 * jax.random.normal(seeds[6], (H * P_SIZE,), jnp.float32), 0.5, 1.5)
    queries = draw_queries(jax.random.fold_in(seeds[18], 71), 0)
    keys_new = draw_keys_new(jax.random.fold_in(seeds[18], 71), 0)
    values_new = noise(seeds[9], (PROMPT_COUNT, NEW_TOKEN_SLOTS, KVH * HD), 1.0, 6.0, ((0, 2), (1, 4), (2, 4)))
    kv_pool = noise(seeds[10], (POOL_ALL, 2, BLK, KVH * HD), 1.0, 6.0, ((0, 2), (3, 4)))
    state_pool = noise(seeds[11], (SPOOL_ALL, H, PP, N), 1.0, 6.0, ((0, 2), (1, 4)))
    new_len = draw_new_len(jax.random.fold_in(seeds[18], 71), 0)
    cached_blocks = ragged(seeds[13], PROMPT_COUNT, PROMPT_COUNT * MAXB * 3 // 4, MAXB, 2).astype(jnp.int32)
    kv_owner_keys = jax.random.split(jax.random.fold_in(seeds[14], 1), PROMPT_COUNT * MAXB // MAXB)
    kv_owner_turns = jax.random.permutation(jax.random.fold_in(seeds[14], 3), PROMPT_COUNT * MAXB // MAXB)
    kv_owner = jax.vmap(lambda own, number: routed_block(jax.random.fold_in(seeds[14], 2), own, number, MAXB, N_BATCH, 1, CAP, 2))(kv_owner_keys, kv_owner_turns).reshape((PROMPT_COUNT, MAXB, 1))
    kv_slot = set_ends(jax.random.randint(seeds[15], (PROMPT_COUNT, MAXB), 0, POOL_DEV), jax.random.fold_in(seeds[15], 1), 0, POOL_DEV - 1).astype(jnp.int32)
    state_owner_keys = jax.random.split(jax.random.fold_in(seeds[16], 1), PROMPT_COUNT * SPIECES // SPIECES)
    state_owner_turns = jax.random.permutation(jax.random.fold_in(seeds[16], 3), PROMPT_COUNT * SPIECES // SPIECES)
    state_owner = jax.vmap(lambda own, number: routed_block(jax.random.fold_in(seeds[16], 2), own, number, SPIECES, N_BATCH, 1, CAP, 1))(state_owner_keys, state_owner_turns).reshape((PROMPT_COUNT, SPIECES, 1))
    state_slot = set_ends(jax.random.randint(seeds[17], (PROMPT_COUNT, SPIECES), 0, SPOOL_DEV), jax.random.fold_in(seeds[17], 1), 0, SPOOL_DEV - 1).astype(jnp.int32)
    return dict(xs=xs, gate_z=gate_z, b_in=b_in, c_in=c_in, log_decay=log_decay, d_skip=d_skip, norm_gain=norm_gain, queries=queries, keys_new=keys_new, values_new=values_new, kv_pool=kv_pool, state_pool=state_pool, new_len=new_len, cached_blocks=cached_blocks, kv_owner=kv_owner, kv_slot=kv_slot, state_owner=state_owner, state_slot=state_slot)


PRECISE = lax.Precision.HIGHEST
EPSILON = 1e-05
NEGATIVE = -1e+30

def block_scan(state_in, inputs_x, inputs_b, inputs_c, decay_part):
    running = jnp.cumsum(decay_part, axis=0)
    span_here = decay_part.shape[0]
    lower = jnp.arange(span_here)[:, None] >= jnp.arange(span_here)[None, :]
    spread = running.T[:, :, None] - running.T[:, None, :]
    factors = jnp.where(lower[None], jnp.exp(jnp.minimum(spread, 0.0)), 0.0)
    intersections = jnp.dot(inputs_c, inputs_b.T, precision=PRECISE)
    inner = jnp.einsum('hts,shp->thp', factors * intersections[None], inputs_x, precision=PRECISE)
    carried = jnp.einsum('tn,hpn->thp', inputs_c, state_in, precision=PRECISE) * jnp.exp(running)[:, :, None]
    remain = jnp.exp(running[-1][None, :] - running)
    state_out = jnp.exp(running[-1])[:, None, None] * state_in + jnp.einsum('shp,sn->hpn', inputs_x * remain[:, :, None], inputs_b, precision=PRECISE)
    return (state_out, inner + carried)

def reference(xs, gate_z, b_in, c_in, log_decay, d_skip, norm_gain, queries, keys_new, values_new, kv_pool, state_pool, new_len, cached_blocks, kv_owner, kv_slot, state_owner, state_slot):

    def ssm_prompt(bundle):
        inputs, gates, inputs_b, inputs_c, decays, prompt_len, owners, slots = bundle
        valid = (jnp.arange(NEW_TOKEN_SLOTS) < prompt_len).astype(jnp.float32)
        inputs_x = inputs.astype(jnp.float32).reshape(NEW_TOKEN_SLOTS, H, P_SIZE) * valid[:, None, None]
        decay_in = decays * valid[:, None]
        pieces = state_pool[owners * SPOOL_DEV + slots]
        start_state = jnp.transpose(pieces, (1, 0, 2, 3)).reshape(H, P_SIZE, N).astype(jnp.float32)
        block_count = NEW_TOKEN_SLOTS // BQ

        def advance(state, blocked):
            return block_scan(state, blocked[0], blocked[1], blocked[2], blocked[3])
        blocked_all = (inputs_x.reshape(block_count, BQ, H, P_SIZE), inputs_b.astype(jnp.float32).reshape(block_count, BQ, N), inputs_c.astype(jnp.float32).reshape(block_count, BQ, N), decay_in.reshape(block_count, BQ, H))
        unused, outputs = lax.scan(advance, start_state, blocked_all)
        scan_out = outputs.reshape(NEW_TOKEN_SLOTS, H, P_SIZE) + d_skip[None, :, None] * inputs_x
        gated = scan_out * jax.nn.silu(gates.astype(jnp.float32).reshape(NEW_TOKEN_SLOTS, H, P_SIZE))
        square_mean = lax.optimization_barrier(jnp.sum(gated * gated, axis=(1, 2))) / (H * P_SIZE)
        normed = gated * lax.rsqrt(square_mean + EPSILON)[:, None, None] * norm_gain.reshape(H, P_SIZE)
        return (normed * valid[:, None, None]).reshape(NEW_TOKEN_SLOTS, H * P_SIZE).astype(jnp.bfloat16)

    def attention_prompt(bundle):
        query_all, key_fresh, value_fresh, prompt_len, block_total, owners, slots = bundle
        records = kv_pool[owners * POOL_DEV + slots]
        cached_keys = records[:, 0].reshape(MAXB * BLK, KVH, HD)
        cached_values = records[:, 1].reshape(MAXB * BLK, KVH, HD)
        all_keys = jnp.concatenate([cached_keys, key_fresh.reshape(NEW_TOKEN_SLOTS, KVH, HD)], axis=0).astype(jnp.float32)
        all_values = jnp.concatenate([cached_values, value_fresh.reshape(NEW_TOKEN_SLOTS, KVH, HD)], axis=0).astype(jnp.float32)
        cached_usable = jnp.arange(MAXB * BLK) // BLK < block_total
        fresh_pos = jnp.arange(NEW_TOKEN_SLOTS)
        fresh_usable = fresh_pos < prompt_len
        query_blocks = query_all.reshape(NEW_TOKEN_SLOTS // STRETCH, STRETCH, KVH, QH // KVH, HD)

        def query_block(bundle_inner):
            block_queries, start = bundle_inner
            query_pos = start + jnp.arange(STRETCH)
            causal = (fresh_pos[None, :] <= query_pos[:, None]) & fresh_usable[None, :]
            allowed = jnp.concatenate([jnp.broadcast_to(cached_usable[None, :], (STRETCH, MAXB * BLK)), causal], axis=1)
            scores = jnp.einsum('tkgd,skd->kgts', block_queries.astype(jnp.float32), all_keys, precision=PRECISE) * HD ** (-0.5)
            scores = jnp.where(allowed[None, None], scores, NEGATIVE)
            highest = lax.optimization_barrier(jnp.max(scores, axis=-1, keepdims=True))
            probs = jnp.where(allowed[None, None], jnp.exp(scores - highest), 0.0)
            denominator = lax.optimization_barrier(jnp.sum(probs, axis=-1))
            rounded = lax.optimization_barrier(probs.astype(jnp.bfloat16))
            weights = rounded.astype(jnp.float32)
            numerator = jnp.einsum('kgts,skd->kgtd', weights, all_values, precision=PRECISE)
            result = numerator / denominator[..., None]
            result = jnp.transpose(result, (2, 0, 1, 3)).reshape(STRETCH, QH * HD)
            query_valid = (query_pos < prompt_len).astype(jnp.float32)
            return (result * query_valid[:, None]).astype(jnp.bfloat16)
        starts = (jnp.arange(NEW_TOKEN_SLOTS // STRETCH) * STRETCH).astype(jnp.int32)
        return lax.map(query_block, (query_blocks, starts)).reshape(NEW_TOKEN_SLOTS, QH * HD)
    ssm_out = lax.map(ssm_prompt, (xs, gate_z, b_in, c_in, log_decay, new_len, state_owner[:, :, 0], state_slot))
    attn_out = lax.map(attention_prompt, (queries, keys_new, values_new, new_len, cached_blocks, kv_owner[:, :, 0], kv_slot))
    return (ssm_out, attn_out)
```

```python
import functools

import jax
import jax.numpy as jnp
from jax import lax
from jax.experimental import pallas as pl
from jax.experimental.pallas import tpu as pltpu
from jax.sharding import PartitionSpec as P

P_SIZE = 64
HD = 128
CAP = 3
EPSILON = 1e-05
NEGATIVE = -1e30
HIGHEST = lax.Precision.HIGHEST
F32 = jnp.float32
BF16 = jnp.bfloat16
VMEM_LIMIT = 48 * 1024 * 1024

SMEM = pl.BlockSpec(memory_space=pltpu.SMEM)
ANY = pl.BlockSpec(memory_space=pl.ANY)


def params():
    return pltpu.CompilerParams(vmem_limit_bytes=VMEM_LIMIT)


def cost(flops, moved, exps=0):
    return pl.CostEstimate(flops=int(flops), bytes_accessed=int(moved), transcendentals=int(exps))


def mm(a, b, precision=None):
    return jnp.dot(a, b, preferred_element_type=F32, precision=precision)


def mm_nt(a, b):
    return lax.dot_general(a, b, (((1,), (1,)), ((), ())), preferred_element_type=F32)


def mm_tn(a, b):
    return lax.dot_general(a, b, (((0,), (0,)), ((), ())), preferred_element_type=F32)


def split(value, terms):
    parts = []
    rest = value
    for term in range(terms):
        part = rest.astype(BF16)
        parts.append(part)
        if term + 1 < terms:
            rest = rest - part.astype(F32)
    return jnp.concatenate(parts, axis=1)


def spread_matrix(heads, terms, width, first_head):
    row = lax.broadcasted_iota(jnp.int32, (terms * heads, width), 0)
    lane = lax.broadcasted_iota(jnp.int32, (terms * heads, width), 1)
    head = lane // P_SIZE + first_head
    return jnp.where(row % heads == head, 1.0, 0.0).astype(BF16)


def request_kernel(total, kv_owner, kv_slot, st_owner, st_slot, ask, kv_place, st_place):
    me = lax.axis_index("batch")
    for shift in range(total - 1):
        for k in range(2 * CAP):
            ask[shift, k] = 0

    def fill(owner_ref, slot_ref, place_ref, base):
        count = slot_ref.shape[1]

        def entry(e, unused):
            owner = owner_ref[0, e, 0]
            slot = slot_ref[0, e]
            rank = lax.fori_loop(
                0, e, lambda f, n: n + jnp.where(owner_ref[0, f, 0] == owner, 1, 0), jnp.int32(0)
            )
            shift = owner - me
            shift = jnp.where(shift < 0, shift + total, shift)

            @pl.when(shift == 0)
            def _():
                place_ref[0, e] = slot
                place_ref[1, e] = -1

            @pl.when(shift > 0)
            def _():
                ask[shift - 1, base + rank] = slot
                place_ref[0, e] = 0
                place_ref[1, e] = (shift - 1) * CAP + rank

            return unused

        lax.fori_loop(0, count, entry, 0)

    fill(kv_owner, kv_slot, kv_place, 0)
    fill(st_owner, st_slot, st_place, CAP)


def make_requests(total, kv_owner, kv_slot, st_owner, st_slot):
    i32 = jnp.int32
    return pl.pallas_call(
        functools.partial(request_kernel, total),
        out_shape=(
            jax.ShapeDtypeStruct((max(total - 1, 1), 2 * CAP), i32),
            jax.ShapeDtypeStruct((2, kv_slot.shape[1]), i32),
            jax.ShapeDtypeStruct((2, st_slot.shape[1]), i32),
        ),
        in_specs=[SMEM] * 4,
        out_specs=(SMEM,) * 3,
        name="requests",
    )(kv_owner, kv_slot, st_owner, st_slot)


def lookup_kernel(asked, kv_pool, st_pool, kv_out, st_out, sems):
    copies = []
    for k in range(CAP):
        copies.append(pltpu.make_async_copy(st_pool.at[asked[0, CAP + k]], st_out.at[k], sems.at[k]))
    for k in range(CAP):
        copies.append(pltpu.make_async_copy(kv_pool.at[asked[0, k]], kv_out.at[k], sems.at[CAP + k]))
    for copy in copies:
        copy.start()
    for copy in copies:
        copy.wait()


def look_up(asked, kv_pool, st_pool):
    return pl.pallas_call(
        lookup_kernel,
        out_shape=(
            jax.ShapeDtypeStruct((CAP,) + kv_pool.shape[1:], BF16),
            jax.ShapeDtypeStruct((CAP,) + st_pool.shape[1:], BF16),
        ),
        in_specs=[SMEM, ANY, ANY],
        out_specs=(ANY, ANY),
        scratch_shapes=[pltpu.SemaphoreType.DMA((2 * CAP,))],
        name="look_up",
    )(asked, kv_pool, st_pool)


def end_state_kernel(heads, new_len, decay, b_in, xs, end, through, running, remain, lasting, b_t):
    step = pl.program_id(0)
    span = decay.shape[0]
    width = xs.shape[1]
    first = lax.axis_index("seq") * span

    @pl.when(step == 0)
    def _():
        position = first + lax.broadcasted_iota(jnp.int32, (span, 1), 0)
        valid = position < new_len[0]
        dec = jnp.where(valid, decay[...], 0.0)
        row = lax.broadcasted_iota(jnp.int32, (span, span), 0)
        col = lax.broadcasted_iota(jnp.int32, (span, span), 1)
        lower = jnp.where(row >= col, 1.0, 0.0).astype(BF16)
        r3 = mm(lower, split(dec, 3))
        r = r3[:, :heads] + r3[:, heads : 2 * heads] + r3[:, 2 * heads :]
        running[...] = r
        last = r[span - 1 :, :]
        remain[...] = split(jnp.exp(last - r), 2)
        lasting[...] = split(jnp.broadcast_to(jnp.exp(last), (8, heads)), 3)
        b = jnp.where(valid, b_in[...].astype(F32), 0.0)
        b_t[...] = b.T.astype(BF16)

    first_head = step * (width // P_SIZE)
    factor = mm(remain[...], spread_matrix(heads, 2, width, first_head))
    weighted = (xs[...].astype(F32) * factor).astype(BF16)
    end[...] = mm(b_t[...], weighted)
    through[...] = mm(lasting[...], spread_matrix(heads, 3, width, first_head))


def end_state(new_len, decay, b_in, xs):
    span, channels = xs.shape
    heads = decay.shape[1]
    n = b_in.shape[1]
    width = min(512, channels)
    return pl.pallas_call(
        functools.partial(end_state_kernel, heads),
        grid=(channels // width,),
        out_shape=(
            jax.ShapeDtypeStruct((n, channels), F32),
            jax.ShapeDtypeStruct((8, channels), F32),
            jax.ShapeDtypeStruct((span, heads), F32),
        ),
        in_specs=[
            SMEM,
            pl.BlockSpec((span, heads), lambda i: (0, 0)),
            pl.BlockSpec((span, n), lambda i: (0, 0)),
            pl.BlockSpec((span, width), lambda i: (0, i)),
        ],
        out_specs=(
            pl.BlockSpec((n, width), lambda i: (0, i)),
            pl.BlockSpec((8, width), lambda i: (0, i)),
            pl.BlockSpec((span, heads), lambda i: (0, 0)),
        ),
        scratch_shapes=[
            pltpu.VMEM((span, 2 * heads), BF16),
            pltpu.VMEM((8, 3 * heads), BF16),
            pltpu.VMEM((n, span), BF16),
        ],
        compiler_params=params(),
        cost_estimate=cost(2 * span * channels * n, span * channels * 2 + n * channels * 4),
        name="end_state",
    )(new_len, decay, b_in, xs)


def local_scan_kernel(heads, new_len, running, b_in, c_in, xs, d_skip, out, cols, rows, inter):
    step = pl.program_id(0)
    span, width = xs.shape
    first = lax.axis_index("seq") * span
    group = width // P_SIZE
    bq = 128
    blocks = span // bq

    @pl.when(step == 0)
    def _():
        r = running[...]
        for g in range(heads // group):
            cols[g] = r[:, g * group : (g + 1) * group]
        rows[...] = r.T
        position = first + lax.broadcasted_iota(jnp.int32, (span, 1), 0)
        b = jnp.where(position < new_len[0], b_in[...].astype(F32), 0.0).astype(BF16)
        inter[...] = mm_nt(c_in[...], b)

    col = cols[step]
    row = rows[pl.ds(pl.multiple_of(step * group, group), group), :]
    skip = mm(split(d_skip[...], 3), spread_matrix(heads, 3, width, step * group))
    lower = lax.broadcasted_iota(jnp.int32, (bq, bq), 0) >= lax.broadcasted_iota(
        jnp.int32, (bq, bq), 1
    )
    left = lax.broadcasted_iota(jnp.int32, (span, 2 * P_SIZE), 1) < P_SIZE
    for pair in range(group // 2):
        lanes = slice(pair * 2 * P_SIZE, (pair + 1) * 2 * P_SIZE)
        x_pair = xs[:, lanes]
        zero = jnp.zeros_like(x_pair)
        sides = (jnp.where(left, x_pair, zero), jnp.where(left, zero, x_pair))
        for i in range(blocks):
            here = slice(i * bq, (i + 1) * bq)
            lhs, rhs = [], []
            for side in range(2):
                h = pair * 2 + side
                at_t = jnp.broadcast_to(col[here, h : h + 1], (bq, bq))
                for j in range(i + 1):
                    there = slice(j * bq, (j + 1) * bq)
                    gap = at_t - row[h : h + 1, there]
                    if j == i:
                        gap = jnp.where(lower, gap, NEGATIVE)
                    lhs.append((jnp.exp(gap) * inter[here, there]).astype(BF16))
                    rhs.append(sides[side][there])
            y = mm(jnp.concatenate(lhs, axis=1), jnp.concatenate(rhs, axis=0))
            out[here, lanes] = y + skip[:1, lanes] * x_pair[here].astype(F32)


def local_scan(new_len, running, b_in, c_in, xs, d_skip):
    span, channels = xs.shape
    heads = running.shape[1]
    n = b_in.shape[1]
    width = min(512, channels)
    group = width // P_SIZE
    whole = lambda *shape: pl.BlockSpec(shape, lambda i: (0,) * len(shape))
    return pl.pallas_call(
        functools.partial(local_scan_kernel, heads),
        grid=(channels // width,),
        out_shape=jax.ShapeDtypeStruct((span, channels), F32),
        in_specs=[
            SMEM,
            whole(span, heads),
            whole(span, n),
            whole(span, n),
            pl.BlockSpec((span, width), lambda i: (0, i)),
            whole(1, heads),
        ],
        out_specs=pl.BlockSpec((span, width), lambda i: (0, i)),
        scratch_shapes=[
            pltpu.VMEM((heads // group, span, group), F32),
            pltpu.VMEM((heads, span), F32),
            pltpu.VMEM((span, span), F32),
        ],
        compiler_params=params(),
        cost_estimate=cost(
            2 * span * span * channels, span * channels * 6, span * span * heads // 2
        ),
        name="local_scan",
    )(new_len, running, b_in, c_in, xs, d_skip)


def start_kernel(pieces, place, pool, received, end, through, start, state, gathered, sems):
    here = lax.axis_index("seq") == 0

    @pl.when(here)
    def _():
        for j in range(pieces):
            slot, taken = place[0, j], place[1, j]

            @pl.when(taken < 0)
            def _():
                pltpu.make_async_copy(pool.at[slot], gathered.at[j], sems.at[j]).start()

            @pl.when(taken >= 0)
            def _():
                pltpu.make_async_copy(received.at[taken], gathered.at[j], sems.at[j]).start()

        for j in range(pieces):
            pltpu.make_async_copy(pool.at[0], gathered.at[j], sems.at[j]).wait()
        heads = gathered.shape[1]
        for h in range(0, heads, 2):
            parts = [gathered[j, h + k] for k in range(2) for j in range(pieces)]
            block = jnp.concatenate(parts, axis=0).astype(F32).T
            lanes = slice(h * P_SIZE, (h + 2) * P_SIZE)
            start[:, lanes] = block.astype(BF16)
            state[:, lanes] = (through[:1, lanes] * block + end[:, lanes]).astype(BF16)


def start_state(place, pool, received, end, through):
    n, channels = end.shape
    pieces = place.shape[1]
    shape = jax.ShapeDtypeStruct((n, channels), BF16)
    whole = pl.BlockSpec(memory_space=pltpu.VMEM)
    return pl.pallas_call(
        functools.partial(start_kernel, pieces),
        out_shape=(shape, shape),
        in_specs=[SMEM, ANY, ANY, whole, whole],
        out_specs=(whole, whole),
        scratch_shapes=[
            pltpu.VMEM((pieces,) + pool.shape[1:], BF16),
            pltpu.SemaphoreType.DMA((pieces,)),
        ],
        compiler_params=params(),
        cost_estimate=cost(n * channels * 4, n * channels * 8),
        name="start_state",
    )(place, pool, received, end, through)


def assembled_start(place, pool, received):
    local = pool[place[0]]
    taken = received[jnp.maximum(place[1], 0)]
    pieces = jnp.where((place[1] < 0)[:, None, None, None], local, taken)
    pieces = jnp.transpose(pieces, (1, 0, 2, 3))
    heads = pieces.shape[0]
    return pieces.reshape(heads * P_SIZE, pieces.shape[-1]).T


def advance_kernel(turn, state_in, end, through, state):
    @pl.when(lax.axis_index("seq") == turn)
    def _():
        state[...] = (through[:1, :] * state_in[...].astype(F32) + end[...]).astype(BF16)


def advance(turn, state_in, end, through):
    n, channels = end.shape
    whole = pl.BlockSpec(memory_space=pltpu.VMEM)
    return pl.pallas_call(
        functools.partial(advance_kernel, turn),
        out_shape=jax.ShapeDtypeStruct((n, channels), BF16),
        in_specs=[whole] * 3,
        out_specs=whole,
        compiler_params=params(),
        cost_estimate=cost(n * channels * 2, n * channels * 8),
        name="advance_state",
    )(state_in, end, through)


def gate_kernel(heads, running, c_in, local, gate, *rest):
    states = rest[:4]
    gated, squares, incoming, factors, summed, sem = rest[4:]
    step = pl.program_id(0)
    span, width = local.shape
    seq = lax.axis_index("seq")

    @pl.when(step == 0)
    def _():
        for turn in range(4):

            @pl.when(seq == turn)
            def _():
                pltpu.make_async_copy(states[turn], incoming, sem).start()

        factors[...] = split(jnp.exp(running[...]), 3)
        summed[...] = jnp.zeros_like(summed)
        pltpu.make_async_copy(states[0], incoming, sem).wait()

    factor = mm(factors[...], spread_matrix(heads, 3, width, step * (width // P_SIZE)))
    lanes = pl.ds(pl.multiple_of(step * width, width), width)
    carried = mm(c_in[...], incoming[:, lanes])
    z = gate[...].astype(F32)
    value = (local[...] + factor * carried) * (z / (1.0 + jnp.exp(-z)))
    gated[...] = value
    square = value * value
    total = square[:, :128]
    for k in range(1, width // 128):
        total = total + square[:, k * 128 : (k + 1) * 128]
    summed[...] += total

    @pl.when(step == pl.num_programs(0) - 1)
    def _():
        ones = jnp.ones((8, 128), F32)
        squares[...] = lax.dot_general(
            ones, summed[...], (((1,), (1,)), ((), ())), precision=HIGHEST, preferred_element_type=F32
        )


def gate_output(running, c_in, local, gate, states):
    span, channels = local.shape
    heads = running.shape[1]
    n = c_in.shape[1]
    width = min(512, channels)
    return pl.pallas_call(
        functools.partial(gate_kernel, heads),
        grid=(channels // width,),
        out_shape=(
            jax.ShapeDtypeStruct((span, channels), F32),
            jax.ShapeDtypeStruct((8, span), F32),
        ),
        in_specs=[
            pl.BlockSpec((span, heads), lambda i: (0, 0)),
            pl.BlockSpec((span, n), lambda i: (0, 0)),
            pl.BlockSpec((span, width), lambda i: (0, i)),
            pl.BlockSpec((span, width), lambda i: (0, i)),
        ]
        + [ANY] * 4,
        out_specs=(
            pl.BlockSpec((span, width), lambda i: (0, i)),
            pl.BlockSpec((8, span), lambda i: (0, 0)),
        ),
        scratch_shapes=[
            pltpu.VMEM((n, channels), BF16),
            pltpu.VMEM((span, 3 * heads), BF16),
            pltpu.VMEM((span, 128), F32),
            pltpu.SemaphoreType.DMA,
        ],
        compiler_params=params(),
        cost_estimate=cost(2 * span * channels * n, span * channels * 10, span * channels),
        name="gate",
    )(running, c_in, local, gate, *states)


def norm_kernel(all_channels, new_len, gated, gain, *rest):
    sums, out = rest[:-1], rest[-1]
    span = gated.shape[0]
    total = sums[0][...]
    for part in sums[1:]:
        total = total + part[...]
    scale = lax.rsqrt(total / all_channels + EPSILON).T[:, :1]
    position = lax.axis_index("seq") * span + lax.broadcasted_iota(jnp.int32, (span, 1), 0)
    scale = jnp.where(position < new_len[0], scale, 0.0)
    out[...] = (gated[...] * scale * gain[...]).astype(BF16)


def norm_output(new_len, gated, gain, sums, all_channels):
    span, channels = gated.shape
    width = min(512, channels)
    return pl.pallas_call(
        functools.partial(norm_kernel, all_channels),
        grid=(channels // width,),
        out_shape=jax.ShapeDtypeStruct((span, channels), BF16),
        in_specs=[
            SMEM,
            pl.BlockSpec((span, width), lambda i: (0, i)),
            pl.BlockSpec((1, width), lambda i: (0, i)),
        ]
        + [pl.BlockSpec((8, span), lambda i: (0, 0))] * len(sums),
        out_specs=pl.BlockSpec((span, width), lambda i: (0, i)),
        compiler_params=params(),
        cost_estimate=cost(span * channels * 3, span * channels * 6),
        name="norm",
    )(new_len, gated, gain, *sums)


def attention_kernel(
    kv_head, new_len, cached, place, q, own_k, own_v, near, far_a, far_b, pool, received, out,
    cache_k, cache_v, acc, top, sems,
):
    span = q.shape[0]
    groups = q.shape[1] // HD
    entries = place.shape[1]
    rows_each = pool.shape[2]
    seq = lax.axis_index("seq")
    scale = HD ** (-0.5)
    lanes = pl.ds(kv_head * HD, HD)
    for e in range(entries):
        slot, taken = place[0, e], place[1, e]
        rows = pl.ds(e * rows_each, rows_each)
        for which, target in ((0, cache_k), (1, cache_v)):

            @pl.when(taken < 0)
            def _():
                pltpu.make_async_copy(
                    pool.at[slot, which, :, lanes], target.at[rows], sems.at[which, e]
                ).start()

            @pl.when(taken >= 0)
            def _():
                pltpu.make_async_copy(
                    received.at[taken, which, :, lanes], target.at[rows], sems.at[which, e]
                ).start()

    bq = 128
    blocks = span // bq

    def widened(v):
        return jnp.concatenate([v, jnp.ones_like(v)], axis=1)

    lower = lax.broadcasted_iota(jnp.int32, (bq, bq), 0) >= lax.broadcasted_iota(
        jnp.int32, (bq, bq), 1
    )
    for g in range(groups):
        for i in range(blocks):
            here = slice(i * bq, (i + 1) * bq)
            s = mm_nt(q[here, g * HD : (g + 1) * HD], own_k[: (i + 1) * bq, :]) * scale
            tail = jnp.where(lower, s[:, i * bq :], NEGATIVE)
            s = tail if i == 0 else jnp.concatenate([s[:, : i * bq], tail], axis=1)
            high = jnp.max(s, axis=1, keepdims=True)
            p = jnp.exp(s - high).astype(BF16)
            at = slice(g * span + i * bq, g * span + (i + 1) * bq)
            acc[at] = mm(p, widened(own_v[: (i + 1) * bq, :]))
            top[at] = jnp.broadcast_to(high, (bq, HD))

    def absorb(keys, values, mask=None):
        values = widened(values)
        for g in range(groups):
            for i in range(blocks):
                here = slice(i * bq, (i + 1) * bq)
                at = slice(g * span + i * bq, g * span + (i + 1) * bq)
                s = mm_nt(q[here, g * HD : (g + 1) * HD], keys) * scale
                if mask is not None:
                    s = jnp.where(mask, s, NEGATIVE)
                before = top[at]
                high = jnp.maximum(before[:, :1], jnp.max(s, axis=1, keepdims=True))
                p = jnp.exp(s - high).astype(BF16)
                shrink = jnp.exp(before - high)
                acc[at] = acc[at] * jnp.concatenate([shrink, shrink], axis=1) + mm(p, values)
                top[at] = jnp.broadcast_to(high, (bq, HD))

    @pl.when(seq % 2 == 1)
    def _():
        absorb(near[0], near[1])

    for e in range(entries):
        for which, target in ((0, cache_k), (1, cache_v)):
            rows = pl.ds(e * rows_each, rows_each)
            pltpu.make_async_copy(
                pool.at[0, which, :, lanes], target.at[rows], sems.at[which, e]
            ).wait()
    portion = min(entries, 4) * rows_each

    def cached_portion(k, unused):
        begin = k * portion
        rows = pl.ds(pl.multiple_of(begin, portion), portion)
        key = begin + lax.broadcasted_iota(jnp.int32, (bq, portion), 1)
        absorb(cache_k[rows, :], cache_v[rows, :], key < cached[0] * rows_each)
        return unused

    if entries * rows_each == portion:
        cached_portion(0, 0)
    else:
        lax.fori_loop(0, entries * rows_each // portion, cached_portion, 0)

    @pl.when(seq >= 2)
    def _():
        absorb(far_a[0], far_a[1])
        absorb(far_b[0], far_b[1])

    position = seq * span + lax.broadcasted_iota(jnp.int32, (span, 1), 0)
    valid = position < new_len[0]
    for g in range(groups):
        at = slice(g * span, (g + 1) * span)
        ratio = acc[at, :HD] / acc[at, HD:]
        out[:, g * HD : (g + 1) * HD] = jnp.where(valid, ratio, 0.0).astype(BF16)


def attention(kv_head, new_len, cached, place, q, keys, values, near, far_a, far_b, pool, received):
    span = q.shape[0]
    kv_heads = keys.shape[1] // HD
    width = q.shape[1] // kv_heads
    entries = place.shape[1]
    rows_each = pool.shape[2]
    groups = width // HD
    pick = pl.BlockSpec((span, HD), lambda i: (0, kv_head))
    pick2 = pl.BlockSpec((2, span, HD), lambda i: (0, 0, kv_head))
    return pl.pallas_call(
        functools.partial(attention_kernel, kv_head),
        grid=(1,),
        out_shape=jax.ShapeDtypeStruct((span, width), BF16),
        in_specs=[
            SMEM,
            SMEM,
            SMEM,
            pl.BlockSpec((span, width), lambda i: (0, kv_head)),
            pick,
            pick,
            pick2,
            pick2,
            pick2,
            ANY,
            ANY,
        ],
        out_specs=pl.BlockSpec((span, width), lambda i: (0, 0)),
        scratch_shapes=[
            pltpu.VMEM((entries * rows_each, HD), BF16),
            pltpu.VMEM((entries * rows_each, HD), BF16),
            pltpu.VMEM((groups * span, 2 * HD), F32),
            pltpu.VMEM((groups * span, HD), F32),
            pltpu.SemaphoreType.DMA((2, entries)),
        ],
        compiler_params=params(),
        cost_estimate=cost(
            4 * groups * span * 1792 * HD, span * width * 4 + 4 * span * HD * 4, groups * span * 1792
        ),
        name="attention",
    )(new_len, cached, place, q, keys, values, near, far_a, far_b, pool, received)


def per_device(
    xs, gate_z, b_in, c_in, log_decay, d_skip, norm_gain, queries, keys_new, values_new, kv_pool,
    state_pool, new_len, cached_blocks, kv_owner, kv_slot, state_owner, state_slot,
):
    total = lax.axis_size("batch")
    channels_all = xs.shape[2] * lax.axis_size("mp")
    xs, gate_z, b_in, c_in, decay = xs[0], gate_z[0], b_in[0], c_in[0], log_decay[0]
    queries, keys_new, values_new = queries[0], keys_new[0], values_new[0]

    fresh = jnp.stack([keys_new, values_new])
    far_a = lax.ppermute(fresh, "seq", [(0, 2), (1, 3)])
    near = lax.ppermute(fresh, "seq", [(0, 1), (2, 3)])

    ask, kv_place, st_place = make_requests(total, kv_owner, kv_slot, state_owner, state_slot)
    kv_received, st_received = [], []
    for shift in range(1, total):
        there = [(i, (i + shift) % total) for i in range(total)]
        back = [(j, i) for i, j in there]
        asked = lax.ppermute(ask[shift - 1 : shift], "batch", there)
        kv_found, st_found = look_up(asked, kv_pool, state_pool)
        st_received.append(lax.ppermute(st_found, "batch", back))
        kv_received.append(lax.ppermute(kv_found, "batch", back))
    if total > 2:
        kv_received = jnp.concatenate(kv_received, axis=0)
        st_received = jnp.concatenate(st_received, axis=0)
    else:
        kv_received, st_received = kv_received[0], st_received[0]

    end, through, running = end_state(new_len, decay, b_in, xs)
    local = local_scan(new_len, running, b_in, c_in, xs, d_skip[None])

    if state_pool.shape[2] % 16 == 0:
        start, state = start_state(st_place, state_pool, st_received, end, through)
    else:
        start = assembled_start(st_place, state_pool, st_received)
        state = advance(0, start, end, through)
    states = [start]
    far_b = lax.ppermute(far_a, "seq", [(2, 3), (3, 2)])
    states.append(lax.ppermute(state, "seq", [(0, 1)]))
    state = advance(1, states[1], end, through)
    states.append(lax.ppermute(state, "seq", [(1, 2)]))
    state = advance(2, states[2], end, through)
    states.append(lax.ppermute(state, "seq", [(2, 3)]))

    kv_heads = keys_new.shape[1] // HD
    attended = [
        attention(
            head, new_len, cached_blocks, kv_place, queries, keys_new, values_new, near, far_a,
            far_b, kv_pool, kv_received,
        )
        for head in range(kv_heads)
    ]

    gated, squares = gate_output(running, c_in, local, gate_z, states)
    sums = [squares]
    mp = lax.axis_size("mp")
    for shift in range(1, mp):
        sums.append(lax.ppermute(squares, "mp", [(i, (i + shift) % mp) for i in range(mp)]))
    ssm_out = norm_output(new_len, gated, norm_gain[None], sums, channels_all)
    return (ssm_out[None], jnp.concatenate(attended, axis=1)[None])


def solution(mesh):
    in_specs = (
        P("batch", "seq", "mp"),
        P("batch", "seq", "mp"),
        P("batch", "seq", None),
        P("batch", "seq", None),
        P("batch", "seq", "mp"),
        P("mp"),
        P("mp"),
        P("batch", "seq", "mp"),
        P("batch", "seq", "mp"),
        P("batch", "seq", "mp"),
        P("batch", None, None, "mp"),
        P("batch", "mp", None, None),
        P("batch"),
        P("batch"),
        P("batch", None, None),
        P("batch", None),
        P("batch", None, None),
        P("batch", None),
    )
    out_specs = (P("batch", "seq", "mp"), P("batch", "seq", "mp"))
    return jax.shard_map(
        per_device, mesh=mesh, in_specs=in_specs, out_specs=out_specs, check_vma=False
    )
```

```python
import functools

import jax
import jax.numpy as jnp
from jax import lax
from jax.experimental import pallas as pl
from jax.experimental.pallas import tpu as pltpu
from jax.sharding import PartitionSpec as P

P_SIZE = 64
HD = 128
CAP = 3
BQ = 128
EPSILON = 1e-05
NEGATIVE = -1e30
LOG2E = 1.4426950408889634
HIGHEST = lax.Precision.HIGHEST
F32 = jnp.float32
BF16 = jnp.bfloat16

SMEM = pl.BlockSpec(memory_space=pltpu.SMEM)
ANY = pl.BlockSpec(memory_space=pl.ANY)
VMEM = pl.BlockSpec(memory_space=pltpu.VMEM)
HBM = pl.BlockSpec(memory_space=pltpu.HBM)


def call(kernel, name, out, ins, outs, scratch=(), mib=16, aliases=None, after=()):
    count = len(ins)

    def body(*refs):
        kernel(*refs[:count], *refs[count + len(after) :])

    run = pl.pallas_call(
        body,
        out_shape=out,
        in_specs=list(ins) + [ANY] * len(after),
        out_specs=outs,
        scratch_shapes=list(scratch),
        input_output_aliases=aliases or {},
        compiler_params=pltpu.CompilerParams(vmem_limit_bytes=mib * 1024 * 1024),
        cost_estimate=pl.CostEstimate(flops=10**10, bytes_accessed=10**7, transcendentals=0),
        name=name,
    )
    return lambda *operands: run(*operands, *after)


def struct(*shape, dtype=F32):
    return jax.ShapeDtypeStruct(shape, dtype)


def mm(a, b):
    return jnp.dot(a, b, preferred_element_type=F32)


def mm_nt(a, b):
    return lax.dot_general(a, b, (((1,), (1,)), ((), ())), preferred_element_type=F32)


def split(value, terms, axis=1):
    parts = []
    rest = value
    for term in range(terms):
        part = rest.astype(BF16)
        parts.append(part)
        if term + 1 < terms:
            rest = rest - part.astype(F32)
    return jnp.concatenate(parts, axis=axis)


def spread_matrix(heads, terms, first_head, width):
    row = lax.broadcasted_iota(jnp.int32, (heads, width), 0)
    lane = lax.broadcasted_iota(jnp.int32, (heads, width), 1)
    one = jnp.where(row == (lane >> 6) + first_head, 1.0, 0.0).astype(BF16)
    return jnp.concatenate([one] * terms, axis=0)


def valid_rows(new_len, span):
    position = lax.axis_index("seq") * span + lax.broadcasted_iota(jnp.int32, (span, 1), 0)
    return position < new_len[0]


def slots_of(lists, base, count, owner):
    found, seen = [jnp.int32(0)] * CAP, jnp.int32(0)
    for e in range(count):
        match = lists[base + e] == owner
        slot = lists[base + count + e]
        found = [jnp.where(match & (seen == k), slot, at) for k, at in enumerate(found)]
        seen = seen + match.astype(jnp.int32)
    return found


def place_of(lists, base, count, e, total):
    owner = lists[base + e]
    shift = owner - lax.axis_index("batch")
    shift = jnp.where(shift < 0, shift + total, shift)
    rank = lax.fori_loop(
        0, e, lambda f, n: n + (lists[base + f] == owner).astype(jnp.int32), jnp.int32(0)
    )
    mine = shift == 0
    taken = (shift - 1) * CAP + jnp.minimum(rank, CAP - 1)
    return mine, jnp.where(mine, 0, taken)


def lookup_kernel(entries, pieces, asked, lists, kv_pool, st_pool, *outs):
    me = lax.axis_index("batch")
    for k, slot in enumerate(slots_of(asked, 0, entries, me)):
        outs[0][k] = kv_pool[slot]
    for k, slot in enumerate(slots_of(asked, 2 * entries, pieces, me)):
        outs[1][k] = st_pool[slot]
    if len(outs) > 2:
        for e in range(entries):
            outs[2][e] = kv_pool[lists[entries + e]]
        for e in range(pieces):
            outs[3][e] = st_pool[lists[2 * entries + pieces + e]]


def look_up(asked, lists, entries, pieces, kv_pool, st_pool, own, after):
    kv, st = kv_pool.shape[1:], st_pool.shape[1:]
    out = [struct(CAP, *kv, dtype=BF16), struct(CAP, *st, dtype=BF16)]
    if own:
        out += [struct(entries, *kv, dtype=BF16), struct(pieces, *st, dtype=BF16)]
    return call(
        functools.partial(lookup_kernel, entries, pieces),
        "look_up",
        tuple(out),
        [SMEM, SMEM, VMEM, VMEM],
        (VMEM,) * len(out),
        after=after,
    )(asked, lists, kv_pool, st_pool)


def zeros_kernel(out):
    out[...] = jnp.zeros_like(out)


def zeros(count):
    return call(zeros_kernel, "zeros", struct(1, count, dtype=jnp.int32), [], VMEM)()[0]


def laid_kernel(count, *refs):
    out = refs[count]
    begin = 0
    for ref in refs[:count]:
        if len(ref.shape) == 2:
            out[begin] = ref[...]
            begin += 1
        else:
            out[begin : begin + ref.shape[0]] = ref[...]
            begin += ref.shape[0]


def laid_together(parts, after):
    rows = sum(part.shape[0] if part.ndim == 3 else 1 for part in parts)
    return call(
        functools.partial(laid_kernel, len(parts)),
        "laid_together",
        struct(rows, *parts[0].shape[-2:], dtype=BF16),
        [VMEM] * len(parts),
        VMEM,
        after=after,
    )(*parts)


def end_state_kernel(new_len, decay_t, b_in, xs, sent, end, through, running, running_t):
    span, channels = xs.shape
    heads = decay_t.shape[0]
    n = b_in.shape[1]
    lane = lax.axis_index("seq") * span + lax.broadcasted_iota(jnp.int32, (1, span), 1)
    dec = jnp.where(lane < new_len[0], decay_t[...], 0.0)
    row = lax.broadcasted_iota(jnp.int32, (span, span), 0)
    col = lax.broadcasted_iota(jnp.int32, (span, span), 1)
    upper = jnp.where(row <= col, 1.0, 0.0).astype(BF16)
    r3 = mm(split(dec, 3, 0), upper)
    r_t = r3[:heads] + r3[heads : 2 * heads] + r3[2 * heads :]
    running_t[...] = r_t
    r = r_t.T
    running[...] = r
    last = r[span - 1 :, :]
    remain = split(jnp.exp(last - r), 2)
    lasting = split(jnp.broadcast_to(jnp.exp(last), (8, heads)), 3)
    b_t = jnp.where(valid_rows(new_len, span), b_in[...].astype(F32), 0.0).T.astype(BF16)
    width = min(512, channels)
    for begin in range(0, channels, width):
        lanes = slice(begin, begin + width)
        spread = spread_matrix(heads, 3, begin // P_SIZE, width)
        factor = mm(remain, spread[: 2 * heads])
        weighted = (xs[:, lanes].astype(F32) * factor).astype(BF16)
        state = mm(b_t, weighted)
        end[:, lanes] = state
        sent[:n, lanes] = state.astype(BF16)
        whole = mm(lasting, spread)
        through[:, lanes] = whole
        sent[n:, lanes] = jnp.concatenate(
            [split(whole[:1], 3, 0), jnp.zeros((13, width), BF16)], axis=0
        )


def end_state(new_len, decay_t, b_in, xs, after):
    span, channels = xs.shape
    heads = decay_t.shape[0]
    n = b_in.shape[1]
    return call(
        end_state_kernel,
        "end_state",
        (
            struct(n + 16, channels, dtype=BF16),
            struct(n, channels),
            struct(8, channels),
            struct(span, heads),
            struct(heads, span),
        ),
        [SMEM, VMEM, VMEM, VMEM],
        (VMEM,) * 5,
        after=after,
    )(new_len, decay_t, b_in, xs)


def local_scan_kernel(
    begin, new_len, running, running_t, b_in, c_in, xs, d_skip, out, cols, inter, skips
):
    span, channels = xs.shape
    heads = running.shape[1]
    here_channels = out.shape[1]
    width = min(512, here_channels)
    group = width // P_SIZE
    blocks = span // BQ
    r = running[...]
    for g in range(here_channels // width):
        first = begin // P_SIZE + g * group
        cols[g] = r[:, first : first + group]
    b = jnp.where(valid_rows(new_len, span), b_in[...].astype(F32), 0.0).astype(BF16)
    inter[...] = mm_nt(c_in[...], b)
    spread = spread_matrix(heads, 3, begin // P_SIZE, here_channels)
    skips[...] = mm(split(jnp.broadcast_to(d_skip[...], (8, heads)), 3), spread)
    lower = lax.broadcasted_iota(jnp.int32, (BQ, BQ), 0) >= lax.broadcasted_iota(
        jnp.int32, (BQ, BQ), 1
    )
    left = lax.broadcasted_iota(jnp.int32, (span, 2 * P_SIZE), 1) < P_SIZE

    def heads_of(step, unused):
        col = cols[step]
        row = running_t[pl.ds(pl.multiple_of(begin // P_SIZE + step * group, group), group), :]
        for pair in range(group // 2):
            offset = step * width + pair * 2 * P_SIZE
            lanes = pl.ds(pl.multiple_of(offset, 2 * P_SIZE), 2 * P_SIZE)
            x_pair = xs[:, pl.ds(pl.multiple_of(begin + offset, 2 * P_SIZE), 2 * P_SIZE)]
            zero = jnp.zeros_like(x_pair)
            sides = (jnp.where(left, x_pair, zero), jnp.where(left, zero, x_pair))
            for i in range(blocks):
                here = slice(i * BQ, (i + 1) * BQ)
                lhs, rhs = [], []
                for side in range(2):
                    h = pair * 2 + side
                    at_t = jnp.broadcast_to(col[here, h : h + 1], (BQ, BQ))
                    for j in range(i + 1):
                        there = slice(j * BQ, (j + 1) * BQ)
                        gap = at_t - row[h : h + 1, there]
                        if j == i:
                            gap = jnp.where(lower, gap, NEGATIVE)
                        lhs.append((jnp.exp(gap) * inter[here, there]).astype(BF16))
                        rhs.append(sides[side][there])
                y = mm(jnp.concatenate(lhs, axis=1), jnp.concatenate(rhs, axis=0))
                out[here, lanes] = y + skips[:1, lanes] * x_pair[here].astype(F32)
        return unused

    lax.fori_loop(0, here_channels // width, heads_of, 0)


def local_scan(begin, size, operands, after):
    span = operands[-2].shape[0]
    width = min(512, size)
    return call(
        functools.partial(local_scan_kernel, begin),
        "local_scan",
        struct(span, size),
        [SMEM] + [VMEM] * 6,
        VMEM,
        [
            pltpu.VMEM((size // width, span, width // P_SIZE), F32),
            pltpu.VMEM((span, span), F32),
            pltpu.VMEM((8, size), F32),
        ],
        after=after,
    )(*operands)


def kept_factors(sent, n, lanes=slice(None)):
    return jnp.sum(sent[n : n + 16, lanes].astype(F32), axis=0, keepdims=True)


def middle_kernel(received, end, through, sent):
    seq = lax.axis_index("seq")
    n, channels = end.shape
    half = channels // 2

    def combine(lanes, early_e, early_t, late_e, late_t):
        sent[:n, :] = (late_t * early_e[:n, lanes].astype(F32) + late_e[:n, lanes]).astype(BF16)
        rest = jnp.zeros((13, half), BF16)
        sent[n:, :] = jnp.concatenate([split(late_t * early_t, 3, 0), rest], axis=0)

    @pl.when(seq == 0)
    def _():
        lanes = slice(0, half)
        combine(lanes, end, through[:1, lanes], received, kept_factors(received, n, lanes))

    @pl.when(seq == 1)
    def _():
        lanes = slice(half, channels)
        combine(lanes, received, kept_factors(received, n, lanes), end, through[:1, lanes])


def middle_state(received, end, through, after):
    return call(
        middle_kernel,
        "middle_state",
        struct(received.shape[0], received.shape[1] // 2, dtype=BF16),
        [VMEM] * 3,
        VMEM,
        after=after,
    )(received, end, through)


def cached_kernel(base, total, lists, kept_in, taken_in, out):
    pieces, heads = kept_in.shape[:2]
    places = [place_of(lists, base, pieces, j, total) for j in range(pieces)]
    for h in range(0, heads, 2):
        parts = [
            jnp.where(mine, kept_in[j, h + k], taken_in[taken, h + k])
            for k in range(2)
            for j, (mine, taken) in enumerate(places)
        ]
        lanes = slice(h * P_SIZE, (h + 2) * P_SIZE)
        out[:, lanes] = jnp.concatenate(parts, axis=0).astype(F32).T.astype(BF16)


def cached_state(lists, base, total, kept, received, after):
    pieces, heads, rows, n = kept.shape
    channels = heads * pieces * rows
    if rows % 16 == 0:
        return call(
            functools.partial(cached_kernel, base, total),
            "cached_state",
            struct(n, channels, dtype=BF16),
            [SMEM, VMEM, VMEM],
            VMEM,
            after=after,
        )(lists, kept, received)
    owners = lists[base : base + pieces]
    shift = (owners - lax.axis_index("batch")) % total
    order = jnp.arange(pieces)
    same = (owners[:, None] == owners[None, :]) & (order[:, None] > order[None, :])
    rank = jnp.minimum(jnp.sum(same.astype(jnp.int32), axis=1), CAP - 1)
    mine = shift == 0
    taken = received[jnp.where(mine, 0, (shift - 1) * CAP + rank)]
    found = jnp.where(mine[:, None, None, None], kept, taken)
    return jnp.transpose(found, (3, 1, 0, 2)).reshape(n, channels)


def gate_kernel(count, running, c_in, gate, cached, met, middle, swapped, *rest):
    locals_in, (gated, squares) = rest[:count], rest[count:]
    span, channels = gate.shape
    heads = running.shape[1]
    n = c_in.shape[1]
    width = 256
    seq = lax.axis_index("seq")
    far, odd = seq >= 2, seq % 2 == 1

    def entering(begin):
        state = cached[:, begin : begin + width].astype(F32)
        side, at = divmod(begin, channels // 2)
        lanes = slice(at, at + width)
        part = jnp.where(odd == (side == 1), middle[:, lanes], swapped[:, lanes])
        kept = jnp.where(far, kept_factors(part, n), 1.0)
        state = kept * state + jnp.where(far, part[:n].astype(F32), 0.0)
        lanes = slice(begin, begin + width)
        kept = jnp.where(odd, kept_factors(met, n, lanes), 1.0)
        state = kept * state + jnp.where(odd, met[:n, lanes].astype(F32), 0.0)
        return state.astype(BF16)

    factors = split(jnp.exp(running[...]), 2)
    c = c_in[...]
    total = jnp.zeros((span, 128), F32)
    begin = 0
    for local in locals_in:
        for at in range(0, local.shape[1], width):
            lanes = slice(begin + at, begin + at + width)
            factor = mm(factors, spread_matrix(heads, 2, (begin + at) // P_SIZE, width))
            carried = mm(c, entering(begin + at))
            z = gate[:, lanes].astype(F32)
            value = (local[:, at : at + width] + factor * carried) * (z / (1.0 + jnp.exp(-z)))
            gated[:, lanes] = value.astype(BF16)
            square = value * value
            for k in range(width // 128):
                total = total + square[:, k * 128 : (k + 1) * 128]
        begin += local.shape[1]
    ones = jnp.ones((8, 128), F32)
    squares[...] = lax.dot_general(
        ones, total, (((1,), (1,)), ((), ())), precision=HIGHEST, preferred_element_type=F32
    )


def gate_output(running, c_in, gate, cached, met, middle, swapped, local):
    span, channels = gate.shape
    return call(
        functools.partial(gate_kernel, len(local)),
        "gate",
        (struct(span, channels, dtype=BF16), struct(8, span)),
        [VMEM] * (7 + len(local)),
        (VMEM, VMEM),
    )(running, c_in, gate, cached, met, middle, swapped, *local)


def norm_kernel(all_channels, count, new_len, gated, gain, *rest):
    sums, (out, staged, sems) = rest[:count], rest[count:]
    span, channels = gated.shape
    width = min(512, channels)
    total = sums[0][...]
    for part in sums[1:]:
        total = total + part[...]
    scale = lax.rsqrt(total / all_channels + EPSILON).T[:, :1]
    scale = jnp.where(valid_rows(new_len, span), scale, 0.0)
    copies = []
    for k, begin in enumerate(range(0, channels, width)):
        lanes = slice(begin, begin + width)
        staged[:, lanes] = (gated[:, lanes].astype(F32) * scale * gain[:, lanes]).astype(BF16)
        at = pl.ds(begin, width)
        copies.append(pltpu.make_async_copy(staged.at[:, at], out.at[:, at], sems.at[k]))
        copies[-1].start()
    for copy in copies:
        copy.wait()


def norm_output(new_len, gated, gain, sums, all_channels, after):
    span, channels = gated.shape
    return call(
        functools.partial(norm_kernel, all_channels, len(sums)),
        "norm",
        struct(span, channels, dtype=BF16),
        [SMEM] + [VMEM] * (2 + len(sums)),
        HBM,
        [
            pltpu.VMEM((span, channels), BF16),
            pltpu.SemaphoreType.DMA((channels // min(512, channels),)),
        ],
        after=after,
    )(new_len, gated, gain, *sums)


def attention_kernel(
    kv_head, heads, groups, total, new_len, cached, lists, q, own_k, own_v, far, near, kept,
    received, *rest
):
    out, token, keys, values, scores, weights, staged, sems = rest[-8:]
    span = own_k.shape[0]
    entries, rows_each = kept.shape[0], kept.shape[2]
    seq = lax.axis_index("seq")
    lanes = slice(kv_head * HD, (kv_head + 1) * HD)
    cached_len = entries * rows_each
    few = 2 * span + cached_len
    factor = HD ** (-0.5) * LOG2E
    token[...] = jnp.zeros_like(token)

    def put(begin, key_rows, value_rows):
        rows = slice(begin, begin + key_rows.shape[0])
        keys[rows] = key_rows
        values[rows, :HD] = value_rows
        values[rows, HD:] = jnp.ones_like(value_rows)

    put(0, own_k[:, lanes], own_v[:, lanes])
    put(span + cached_len, near[0, :, lanes], near[1, :, lanes])
    for e in range(entries):
        mine, taken = place_of(lists, 0, entries, e, total)
        record = [jnp.where(mine, kept[e, k, :, lanes], received[taken, k, :, lanes]) for k in (0, 1)]
        put(span + e * rows_each, *record)
    key = lax.broadcasted_iota(jnp.int32, (1, few - span), 1)
    open_keys = (key < cached[0] * rows_each) | ((key >= cached_len) & (seq % 2 == 1))
    bias = jnp.where(open_keys, 0.0, NEGATIVE)
    valid = valid_rows(new_len, span)

    def copy_out(k):
        at = pl.ds((kv_head * groups + heads[k]) * HD, HD)
        return pltpu.make_async_copy(staged.at[:, pl.ds(k * HD, HD)], out.at[:, at], sems.at[k])

    def attend(count):
        for k, g in enumerate(heads):
            slot = k % 2
            head = slice((kv_head * groups + g) * HD, (kv_head * groups + g + 1) * HD)
            scores[slot, :, :count] = mm_nt(q[:, head], keys[:count])
            for begin in range(0, span, BQ):
                rows = slice(begin, begin + BQ)
                s = scores[slot, rows, :count]
                at = lax.broadcasted_iota(jnp.int32, (BQ, span), 0) + begin
                past = at >= lax.broadcasted_iota(jnp.int32, (BQ, span), 1)
                parts = [jnp.where(past, s[:, :span], NEGATIVE), s[:, span:few] + bias]
                if count > few:
                    parts.append(s[:, few:])
                s = jnp.concatenate(parts, axis=1)
                high = jnp.max(s, axis=1, keepdims=True)
                weights[slot, rows, :count] = jnp.exp2(s * factor - high * factor).astype(BF16)
            summed = mm(weights[slot, :, :count], values[:count])
            ratio = summed[:, :HD] / summed[:, HD:]
            staged[:, k * HD : (k + 1) * HD] = jnp.where(valid, ratio, 0.0).astype(BF16)
            copy_out(k).start()

    @pl.when(seq < 2)
    def _():
        attend(few)

    @pl.when(seq >= 2)
    def _():
        put(few, far[0, :, lanes], far[1, :, lanes])
        put(few + span, near[2, :, lanes], near[3, :, lanes])
        attend(few + 2 * span)

    for k in range(len(heads)):
        copy_out(k).wait()


def attention(
    kv_head, heads, total, new_len, cached, lists, q, keys, values, far, near, kept,
    received, out, after,
):
    span = q.shape[0]
    groups = q.shape[1] // keys.shape[1]
    most = 4 * span + kept.shape[0] * kept.shape[2]
    operands = (new_len, cached, lists, q, keys, values, far, near, kept, received)
    ins = [SMEM] * 3 + [VMEM] * 7
    aliases = {}
    if out is not None:
        aliases = {len(operands): 0}
        operands += (out,)
        ins += [HBM]
    return call(
        functools.partial(attention_kernel, kv_head, heads, groups, total),
        "attention",
        (struct(*q.shape, dtype=BF16), struct(8, 128)),
        ins,
        (HBM, VMEM),
        [
            pltpu.VMEM((most, HD), BF16),
            pltpu.VMEM((most, 2 * HD), BF16),
            pltpu.VMEM((2, span, most), F32),
            pltpu.VMEM((2, span, most), BF16),
            pltpu.VMEM((span, len(heads) * HD), BF16),
            pltpu.SemaphoreType.DMA((len(heads),)),
        ],
        mib=14 + most * span * 12 // 2**20,
        aliases=aliases,
        after=after,
    )(*operands)


def per_device(
    xs, gate_z, b_in, c_in, log_decay, d_skip, norm_gain, queries, keys_new, values_new, kv_pool,
    state_pool, new_len, cached_blocks, kv_owner, kv_slot, state_owner, state_slot,
):
    total = lax.axis_size("batch")
    mp = lax.axis_size("mp")
    channels_all = xs.shape[2] * mp
    entries, pieces = kv_slot.shape[1], state_slot.shape[1]
    xs, gate_z, b_in, c_in, decay = xs[0], gate_z[0], b_in[0], c_in[0], log_decay[0]
    queries, keys_new, values_new = queries[0], keys_new[0], values_new[0]

    beside = [(0, 1), (1, 0), (2, 3), (3, 2)]
    across = [(0, 2), (1, 3)]

    lists = jnp.concatenate(
        [kv_owner.reshape(-1), kv_slot.reshape(-1), state_owner.reshape(-1), state_slot.reshape(-1)]
    )
    lists = lists + zeros(lists.shape[0])
    fresh = laid_together([keys_new, values_new], (lists,))
    far = lax.ppermute(fresh, "seq", across)
    sent, end, through, running, running_t = end_state(new_len, decay.T, b_in, xs, (fresh,))
    met = lax.ppermute(sent, "seq", beside)

    scan_operands = (new_len, running, running_t, b_in, c_in, xs, d_skip[None])
    half = xs.shape[1] // 2
    kv_received, st_received, kept = [], [], None
    for shift in range(1, total):
        there = [(i, (i + shift) % total) for i in range(total)]
        back = [(j, i) for i, j in there]
        asked = lax.ppermute(lists, "batch", there)
        found = look_up(
            asked, lists, entries, pieces, kv_pool, state_pool, kept is None, (sent,)
        )
        if kept is None:
            kept = found[2:]
        kv_received.append(lax.ppermute(found[0], "batch", back))
        st_received.append(lax.ppermute(found[1], "batch", back))
    if total > 2:
        kv_received = jnp.concatenate(kv_received, axis=0)
        st_received = jnp.concatenate(st_received, axis=0)
    else:
        kv_received, st_received = kv_received[0], st_received[0]
    kv_kept, st_kept = kept

    sent = middle_state(met, end, through, (kv_kept,))
    middle = lax.ppermute(sent, "seq", across)
    both = laid_together([fresh, far], (sent,))
    near = lax.ppermute(both, "seq", beside)

    groups = queries.shape[1] // keys_new.shape[1]
    kv_heads = keys_new.shape[1] // HD

    def attend(kv_head, out, after):
        return attention(
            kv_head, tuple(range(groups)), total, new_len, cached_blocks, lists, queries, keys_new,
            values_new, far, near, kv_kept, kv_received, out, after,
        )

    local = [local_scan(0, half, scan_operands, (both,))]
    local.append(local_scan(half, half // 2, scan_operands, (local[0],)))
    out, token = None, local[1]
    for kv_head in range(kv_heads - 1):
        out, token = attend(kv_head, out, (token,))
    held = laid_together([middle], (token,))
    swapped = lax.ppermute(held, "seq", beside)[0]
    local.append(local_scan(half + half // 2, half // 2, scan_operands, (held,)))
    cached = cached_state(lists, 2 * entries, total, st_kept, st_received, (local[2],))
    gated, squares = gate_output(running, c_in, gate_z, cached, met, middle, swapped, local)
    sums = [squares]
    for shift in range(1, mp):
        sums.append(lax.ppermute(squares, "mp", [(i, (i + shift) % mp) for i in range(mp)]))
    attended, token = attend(kv_heads - 1, out, (squares,))
    ssm_out = norm_output(new_len, gated, norm_gain[None], sums, channels_all, (token,))
    return (ssm_out[None], attended[None])


def solution(mesh):
    in_specs = (
        P("batch", "seq", "mp"),
        P("batch", "seq", "mp"),
        P("batch", "seq", None),
        P("batch", "seq", None),
        P("batch", "seq", "mp"),
        P("mp"),
        P("mp"),
        P("batch", "seq", "mp"),
        P("batch", "seq", "mp"),
        P("batch", "seq", "mp"),
        P("batch", None, None, "mp"),
        P("batch", "mp", None, None),
        P("batch"),
        P("batch"),
        P("batch", None, None),
        P("batch", None),
        P("batch", None, None),
        P("batch", None),
    )
    out_specs = (P("batch", "seq", "mp"), P("batch", "seq", "mp"))
    return jax.shard_map(
        per_device, mesh=mesh, in_specs=in_specs, out_specs=out_specs, check_vma=False
    )
```

```python
import functools

import jax
import jax.numpy as jnp
from jax import lax
from jax.experimental import pallas as pl
from jax.experimental.pallas import tpu as pltpu
from jax.sharding import PartitionSpec as P

P_SIZE = 64
HD = 128
CAP = 3
BQ = 128
NORM_PARTS = 8
EPSILON = 1e-05
NEGATIVE = -1e30
LOG2E = 1.4426950408889634
HIGHEST = lax.Precision.HIGHEST
F32 = jnp.float32
BF16 = jnp.bfloat16

SMEM = pl.BlockSpec(memory_space=pltpu.SMEM)
ANY = pl.BlockSpec(memory_space=pl.ANY)
VMEM = pl.BlockSpec(memory_space=pltpu.VMEM)
HBM = pl.BlockSpec(memory_space=pltpu.HBM)


def call(kernel, name, out, ins, outs, scratch=(), mib=16, after=(), held=(), aliases=None):
    count = len(ins)
    unread = (*after, *held)

    def body(*refs):
        kernel(*refs[:count], *refs[count + len(unread) :])

    run = pl.pallas_call(
        body,
        out_shape=out,
        in_specs=list(ins) + [ANY] * len(after) + [VMEM] * len(held),
        out_specs=outs,
        scratch_shapes=list(scratch),
        input_output_aliases=aliases or {},
        compiler_params=pltpu.CompilerParams(vmem_limit_bytes=mib * 1024 * 1024),
        cost_estimate=pl.CostEstimate(flops=10**10, bytes_accessed=10**7, transcendentals=0),
        name=name,
    )
    return lambda *operands: run(*operands, *unread)


def struct(*shape, dtype=F32):
    return jax.ShapeDtypeStruct(shape, dtype)


def mm(a, b):
    return jnp.dot(a, b, preferred_element_type=F32)


def mm_nt(a, b):
    return lax.dot_general(a, b, (((1,), (1,)), ((), ())), preferred_element_type=F32)


def split(value, terms, axis=1):
    parts = []
    rest = value
    for term in range(terms):
        part = rest.astype(BF16)
        parts.append(part)
        if term + 1 < terms:
            rest = rest - part.astype(F32)
    return jnp.concatenate(parts, axis=axis)


def spread_matrix(heads, terms, first_head, width):
    row = lax.broadcasted_iota(jnp.int32, (heads, width), 0)
    lane = lax.broadcasted_iota(jnp.int32, (heads, width), 1)
    one = jnp.where(row == (lane >> 6) + first_head, 1.0, 0.0).astype(BF16)
    return jnp.concatenate([one] * terms, axis=0)


def valid_rows(new_len, span):
    position = lax.axis_index("seq") * span + lax.broadcasted_iota(jnp.int32, (span, 1), 0)
    return position < new_len[...]


def slots_of(lists, base, count, owner):
    found, seen = [jnp.int32(0)] * CAP, jnp.int32(0)
    for e in range(count):
        match = lists[base + e] == owner
        slot = lists[base + count + e]
        found = [jnp.where(match & (seen == k), slot, at) for k, at in enumerate(found)]
        seen = seen + match.astype(jnp.int32)
    return found


def place_of(lists, base, count, e, total):
    owner = lists[base + e]
    shift = owner - lax.axis_index("batch")
    shift = jnp.where(shift < 0, shift + total, shift)
    rank = lax.fori_loop(
        0, e, lambda f, n: n + (lists[base + f] == owner).astype(jnp.int32), jnp.int32(0)
    )
    mine = shift == 0
    taken = (shift - 1) * CAP + jnp.minimum(rank, CAP - 1)
    return mine, jnp.where(mine, 0, taken)


def lookup_kernel(entries, pieces, asked, lists, kv_pool, st_pool, *outs):
    me = lax.axis_index("batch")
    for k, slot in enumerate(slots_of(asked, 0, entries, me)):
        outs[0][k] = kv_pool[slot]
    for k, slot in enumerate(slots_of(asked, 2 * entries, pieces, me)):
        outs[1][k] = st_pool[slot]
    if len(outs) > 2:
        for e in range(entries):
            outs[2][e] = kv_pool[lists[entries + e]]
        for e in range(pieces):
            outs[3][e] = st_pool[lists[2 * entries + pieces + e]]


def look_up(asked, lists, entries, pieces, kv_pool, st_pool, own, after):
    kv, st = kv_pool.shape[1:], st_pool.shape[1:]
    out = [struct(CAP, *kv, dtype=BF16), struct(CAP, *st, dtype=BF16)]
    if own:
        out += [struct(entries, *kv, dtype=BF16), struct(pieces, *st, dtype=BF16)]
    return call(
        functools.partial(lookup_kernel, entries, pieces),
        "look_up",
        tuple(out),
        [SMEM, SMEM, VMEM, VMEM],
        (VMEM,) * len(out),
        after=after,
    )(asked, lists, kv_pool, st_pool)


def zeros_kernel(out):
    out[...] = jnp.zeros_like(out)


def zeros(count):
    return call(zeros_kernel, "zeros", struct(1, count, dtype=jnp.int32), [], VMEM)()[0]


def laid_kernel(count, *refs):
    out = refs[count]
    begin = 0
    for ref in refs[:count]:
        if len(ref.shape) == 2:
            out[begin] = ref[...]
            begin += 1
        else:
            out[begin : begin + ref.shape[0]] = ref[...]
            begin += ref.shape[0]


def laid_together(parts, after):
    rows = sum(part.shape[0] if part.ndim == 3 else 1 for part in parts)
    return call(
        functools.partial(laid_kernel, len(parts)),
        "laid_together",
        struct(rows, *parts[0].shape[-2:], dtype=BF16),
        [VMEM] * len(parts),
        VMEM,
        after=after,
    )(*parts)


def end_state_kernel(new_len, decay_t, b_in, xs, sent, end, through, running, running_t):
    span, channels = xs.shape
    heads = decay_t.shape[0]
    n = b_in.shape[1]
    lane = lax.axis_index("seq") * span + lax.broadcasted_iota(jnp.int32, (1, span), 1)
    dec = jnp.where(lane < new_len[...], decay_t[...], 0.0)
    row = lax.broadcasted_iota(jnp.int32, (span, span), 0)
    col = lax.broadcasted_iota(jnp.int32, (span, span), 1)
    upper = jnp.where(row <= col, 1.0, 0.0).astype(BF16)
    r3 = mm(split(dec, 3, 0), upper)
    r_t = r3[:heads] + r3[heads : 2 * heads] + r3[2 * heads :]
    running_t[...] = r_t
    r = r_t.T
    running[...] = r
    last = r[span - 1 :, :]
    remain = split(jnp.exp(last - r), 2)
    lasting = split(jnp.broadcast_to(jnp.exp(last), (8, heads)), 3)
    b_t = jnp.where(valid_rows(new_len, span), b_in[...].astype(F32), 0.0).T.astype(BF16)
    width = min(512, channels)
    for begin in range(0, channels, width):
        lanes = slice(begin, begin + width)
        spread = spread_matrix(heads, 3, begin // P_SIZE, width)
        factor = mm(remain, spread[: 2 * heads])
        weighted = (xs[:, lanes].astype(F32) * factor).astype(BF16)
        state = mm(b_t, weighted)
        end[:, lanes] = state
        sent[:n, lanes] = state.astype(BF16)
        whole = mm(lasting, spread)
        through[:, lanes] = whole
        sent[n:, lanes] = jnp.concatenate(
            [split(whole[:1], 3, 0), jnp.zeros((13, width), BF16)], axis=0
        )


def end_state(new_len, decay_t, b_in, xs, after):
    span, channels = xs.shape
    heads = decay_t.shape[0]
    n = b_in.shape[1]
    return call(
        end_state_kernel,
        "end_state",
        (
            struct(n + 16, channels, dtype=BF16),
            struct(n, channels),
            struct(8, channels),
            struct(span, heads),
            struct(heads, span),
        ),
        [VMEM] * 4,
        (VMEM,) * 5,
        after=after,
    )(new_len, decay_t, b_in, xs)


def local_scan_kernel(
    begin, new_len, running, running_t, b_in, c_in, xs, d_skip, out, cols, inter, skips, into, outof
):
    span, channels = xs.shape
    heads = running.shape[1]
    here_channels = out.shape[1]
    width = min(512, here_channels)
    group = width // P_SIZE
    blocks = span // BQ
    r = running[...]
    for g in range(here_channels // width):
        first = begin // P_SIZE + g * group
        cols[g] = r[:, first : first + group]
    for i in range(1, blocks):
        edge = r[i * BQ - 1 : i * BQ, :]
        into[i - 1, : i * BQ] = split(jnp.exp(edge - r[: i * BQ]), 2)
        outof[i - 1] = split(jnp.exp(r[i * BQ : (i + 1) * BQ] - edge), 2)
    b = jnp.where(valid_rows(new_len, span), b_in[...].astype(F32), 0.0).astype(BF16)
    inter[...] = mm_nt(c_in[...], b)
    spread = spread_matrix(heads, 3, begin // P_SIZE, here_channels)
    skips[...] = mm(split(jnp.broadcast_to(d_skip[...], (8, heads)), 3), spread)
    lower = lax.broadcasted_iota(jnp.int32, (BQ, BQ), 0) >= lax.broadcasted_iota(
        jnp.int32, (BQ, BQ), 1
    )
    left = lax.broadcasted_iota(jnp.int32, (span, 2 * P_SIZE), 1) < P_SIZE

    def heads_of(step, unused):
        col = cols[step]
        first = begin // P_SIZE + step * group
        row = running_t[pl.ds(pl.multiple_of(first, group), group), :]
        x_group = xs[:, pl.ds(pl.multiple_of(begin + step * width, width), width)]
        spread = spread_matrix(heads, 2, first, width)
        earlier = [None]
        for i in range(1, blocks):
            factor = mm(into[i - 1, : i * BQ], spread)
            weighted = (x_group[: i * BQ].astype(F32) * factor).astype(BF16)
            product = mm(inter[i * BQ : (i + 1) * BQ, : i * BQ].astype(BF16), weighted)
            earlier.append(product * mm(outof[i - 1], spread))
        for pair in range(group // 2):
            at = slice(pair * 2 * P_SIZE, (pair + 1) * 2 * P_SIZE)
            offset = step * width + pair * 2 * P_SIZE
            lanes = pl.ds(pl.multiple_of(offset, 2 * P_SIZE), 2 * P_SIZE)
            x_pair = x_group[:, at]
            zero = jnp.zeros_like(x_pair)
            sides = (jnp.where(left, x_pair, zero), jnp.where(left, zero, x_pair))
            for i in range(blocks):
                here = slice(i * BQ, (i + 1) * BQ)
                lhs, rhs = [], []
                for side in range(2):
                    h = pair * 2 + side
                    gap = jnp.broadcast_to(col[here, h : h + 1], (BQ, BQ)) - row[h : h + 1, here]
                    gap = jnp.where(lower, gap, NEGATIVE)
                    lhs.append((jnp.exp(gap) * inter[here, here]).astype(BF16))
                    rhs.append(sides[side][here])
                y = mm(jnp.concatenate(lhs, axis=1), jnp.concatenate(rhs, axis=0))
                y = y + skips[:1, lanes] * x_pair[here].astype(F32)
                out[here, lanes] = y if i == 0 else y + earlier[i][:, at]
        return unused

    lax.fori_loop(0, here_channels // width, heads_of, 0)


def local_scan(begin, size, operands, after):
    span = operands[-2].shape[0]
    heads = operands[1].shape[1]
    width = min(512, size)
    blocks = span // BQ
    return call(
        functools.partial(local_scan_kernel, begin),
        "local_scan",
        struct(span, size),
        [VMEM] * 7,
        VMEM,
        [
            pltpu.VMEM((size // width, span, width // P_SIZE), F32),
            pltpu.VMEM((span, span), F32),
            pltpu.VMEM((8, size), F32),
            pltpu.VMEM((blocks - 1, span, 2 * heads), BF16),
            pltpu.VMEM((blocks - 1, BQ, 2 * heads), BF16),
        ],
        after=after,
    )(*operands)


def kept_factors(sent, n, lanes=slice(None)):
    return jnp.sum(sent[n : n + 16, lanes].astype(F32), axis=0, keepdims=True)


def middle_kernel(received, end, through, sent):
    seq = lax.axis_index("seq")
    n, channels = end.shape
    half = channels // 2

    def combine(lanes, early_e, early_t, late_e, late_t):
        sent[:n, :] = (late_t * early_e[:n, lanes].astype(F32) + late_e[:n, lanes]).astype(BF16)
        rest = jnp.zeros((13, half), BF16)
        sent[n:, :] = jnp.concatenate([split(late_t * early_t, 3, 0), rest], axis=0)

    @pl.when(seq == 0)
    def _():
        lanes = slice(0, half)
        combine(lanes, end, through[:1, lanes], received, kept_factors(received, n, lanes))

    @pl.when(seq == 1)
    def _():
        lanes = slice(half, channels)
        combine(lanes, received, kept_factors(received, n, lanes), end, through[:1, lanes])


def middle_state(received, end, through, after):
    return call(
        middle_kernel,
        "middle_state",
        struct(received.shape[0], received.shape[1] // 2, dtype=BF16),
        [VMEM] * 3,
        VMEM,
        after=after,
    )(received, end, through)


def cached_kernel(base, total, lists, kept_in, taken_in, out):
    pieces, heads = kept_in.shape[:2]
    places = [place_of(lists, base, pieces, j, total) for j in range(pieces)]
    for h in range(0, heads, 2):
        parts = [
            jnp.where(mine, kept_in[j, h + k], taken_in[taken, h + k])
            for k in range(2)
            for j, (mine, taken) in enumerate(places)
        ]
        lanes = slice(h * P_SIZE, (h + 2) * P_SIZE)
        out[:, lanes] = jnp.concatenate(parts, axis=0).astype(F32).T.astype(BF16)


def cached_state(lists, base, total, kept, received, after):
    pieces, heads, rows, n = kept.shape
    channels = heads * pieces * rows
    if rows % 16 == 0:
        return call(
            functools.partial(cached_kernel, base, total),
            "cached_state",
            struct(n, channels, dtype=BF16),
            [SMEM, VMEM, VMEM],
            VMEM,
            after=after,
        )(lists, kept, received)
    owners = lists[base : base + pieces]
    shift = (owners - lax.axis_index("batch")) % total
    order = jnp.arange(pieces)
    same = (owners[:, None] == owners[None, :]) & (order[:, None] > order[None, :])
    rank = jnp.minimum(jnp.sum(same.astype(jnp.int32), axis=1), CAP - 1)
    mine = shift == 0
    taken = received[jnp.where(mine, 0, (shift - 1) * CAP + rank)]
    found = jnp.where(mine[:, None, None, None], kept, taken)
    return jnp.transpose(found, (3, 1, 0, 2)).reshape(n, channels)


def gate_kernel(count, running, c_in, gate, cached, met, middle, swapped, *rest):
    locals_in, (gated, squares) = rest[:count], rest[count:]
    span, channels = gate.shape
    heads = running.shape[1]
    n = c_in.shape[1]
    width = 256
    seq = lax.axis_index("seq")
    far, odd = seq >= 2, seq % 2 == 1

    def entering(begin):
        state = cached[:, begin : begin + width].astype(F32)
        side, at = divmod(begin, channels // 2)
        lanes = slice(at, at + width)
        part = jnp.where(odd == (side == 1), middle[:, lanes], swapped[:, lanes])
        kept = jnp.where(far, kept_factors(part, n), 1.0)
        state = kept * state + jnp.where(far, part[:n].astype(F32), 0.0)
        lanes = slice(begin, begin + width)
        kept = jnp.where(odd, kept_factors(met, n, lanes), 1.0)
        state = kept * state + jnp.where(odd, met[:n, lanes].astype(F32), 0.0)
        return state.astype(BF16)

    factors = split(jnp.exp(running[...]), 2)
    c = c_in[...]
    total = jnp.zeros((span, 128), F32)
    begin = 0
    for local in locals_in:
        for at in range(0, local.shape[1], width):
            lanes = slice(begin + at, begin + at + width)
            factor = mm(factors, spread_matrix(heads, 2, (begin + at) // P_SIZE, width))
            carried = mm(c, entering(begin + at))
            z = gate[:, lanes].astype(F32)
            value = (local[:, at : at + width] + factor * carried) * (z / (1.0 + jnp.exp(-z)))
            gated[:, lanes] = value.astype(BF16)
            square = value * value
            for k in range(width // 128):
                total = total + square[:, k * 128 : (k + 1) * 128]
        begin += local.shape[1]
    ones = jnp.ones((8, 128), F32)
    squares[...] = lax.dot_general(
        ones, total, (((1,), (1,)), ((), ())), precision=HIGHEST, preferred_element_type=F32
    )


def gate_output(running, c_in, gate, cached, met, middle, swapped, local):
    span, channels = gate.shape
    return call(
        functools.partial(gate_kernel, len(local)),
        "gate",
        (struct(span, channels, dtype=BF16), struct(8, span)),
        [VMEM] * (7 + len(local)),
        (VMEM, VMEM),
    )(running, c_in, gate, cached, met, middle, swapped, *local)


def norm_kernel(all_channels, count, new_len, gated, gain, late, *rest):
    sums, (out, attended, staged, sems) = rest[:count], rest[count + 1 :]
    span, channels = gated.shape
    rows_each = span // NORM_PARTS
    begin = attended.shape[1] - late.shape[1]
    copies = [
        pltpu.make_async_copy(late, attended.at[:, pl.ds(begin, late.shape[1])], sems.at[0])
    ]
    copies[0].start()
    total = sums[0][...]
    for part in sums[1:]:
        total = total + part[...]
    scale = lax.rsqrt(total / all_channels + EPSILON).T[:, :1]
    scale = jnp.where(valid_rows(new_len, span), scale, 0.0)
    for begin in range(0, span, rows_each):
        rows = slice(begin, begin + rows_each)
        staged[rows] = (gated[rows].astype(F32) * scale[rows] * gain[...]).astype(BF16)
        at = pl.ds(begin, rows_each)
        copies.append(pltpu.make_async_copy(staged.at[at], out.at[at], sems.at[len(copies)]))
        copies[-1].start()
    for copy in copies:
        copy.wait()


def norm_output(new_len, gated, gain, sums, all_channels, late, attended):
    span, channels = gated.shape
    copies = 1 + NORM_PARTS
    return call(
        functools.partial(norm_kernel, all_channels, len(sums)),
        "norm",
        (struct(span, channels, dtype=BF16), struct(*attended.shape, dtype=BF16)),
        [VMEM] * (4 + len(sums)) + [HBM],
        (HBM, HBM),
        [pltpu.VMEM((span, channels), BF16), pltpu.SemaphoreType.DMA((copies,))],
        aliases={4 + len(sums): 1},
    )(new_len, gated, gain, late, *sums, attended)


def attention_kernel(
    heads, groups, total, new_len, cached, lists, q, own_k, own_v, far, near, kept, received, *rest
):
    if len(rest) > 5:
        before, out, staged, keys, values, scores, weights, sem = rest
        done = before.shape[1]
        copy = pltpu.make_async_copy(before, out.at[:, pl.ds(0, done)], sem)
        copy.start()
    else:
        copy = None
        staged, keys, values, scores, weights = rest
    span = own_k.shape[0]
    entries, rows_each = kept.shape[0], kept.shape[2]
    kv_heads = sorted({head // groups for head in heads})
    seq = lax.axis_index("seq")
    cached_len = entries * rows_each
    few = 2 * span + cached_len
    factor = HD ** (-0.5) * LOG2E

    def put(begin, key_rows, value_rows):
        rows = slice(begin, begin + key_rows.shape[0])
        for h, kv_head in enumerate(kv_heads):
            lanes = slice(kv_head * HD, (kv_head + 1) * HD)
            keys[h, rows] = key_rows[:, lanes]
            values[h, rows, :HD] = value_rows[:, lanes]
            values[h, rows, HD:] = jnp.ones_like(value_rows[:, lanes])

    put(0, own_k[...], own_v[...])
    put(span + cached_len, near[0], near[1])
    for e in range(entries):
        mine, taken = place_of(lists, 0, entries, e, total)
        record = [jnp.where(mine, kept[e, k], received[taken, k]) for k in (0, 1)]
        put(span + e * rows_each, *record)
    key = lax.broadcasted_iota(jnp.int32, (1, few - span), 1)
    open_keys = (key < cached[...] * rows_each) | ((key >= cached_len) & (seq % 2 == 1))
    bias = jnp.where(open_keys, 0.0, NEGATIVE)
    valid = valid_rows(new_len, span)

    def attend(count):
        for k, head in enumerate(heads):
            slot, kv_head = k % 2, kv_heads.index(head // groups)
            scores[slot, :, :count] = mm_nt(q[:, head * HD : (head + 1) * HD], keys[kv_head, :count])
            for begin in range(0, span, BQ):
                rows = slice(begin, begin + BQ)
                s = scores[slot, rows, :count]
                at = lax.broadcasted_iota(jnp.int32, (BQ, span), 0) + begin
                past = at >= lax.broadcasted_iota(jnp.int32, (BQ, span), 1)
                parts = [jnp.where(past, s[:, :span], NEGATIVE), s[:, span:few] + bias]
                if count > few:
                    parts.append(s[:, few:])
                s = jnp.concatenate(parts, axis=1)
                high = jnp.max(s, axis=1, keepdims=True)
                weights[slot, rows, :count] = jnp.exp2(s * factor - high * factor).astype(BF16)
            summed = mm(weights[slot, :, :count], values[kv_head, :count])
            ratio = summed[:, :HD] / summed[:, HD:]
            staged[:, k * HD : (k + 1) * HD] = jnp.where(valid, ratio, 0.0).astype(BF16)

    @pl.when(seq < 2)
    def _():
        attend(few)

    @pl.when(seq >= 2)
    def _():
        put(few, far[0], far[1])
        put(few + span, near[2], near[3])
        attend(few + 2 * span)

    if copy is not None:
        copy.wait()


def attention(
    heads, total, new_len, cached, lists, q, keys, values, far, near, kept, received, before, after,
    held,
):
    span = q.shape[0]
    groups = q.shape[1] // keys.shape[1]
    kv_heads = len({head // groups for head in heads})
    most = 4 * span + kept.shape[0] * kept.shape[2]
    operands = [new_len, cached, lists, q, keys, values, far, near, kept, received]
    ins = [VMEM, VMEM, SMEM] + [VMEM] * 7
    out, out_specs = struct(span, len(heads) * HD, dtype=BF16), VMEM
    scratch = [
        pltpu.VMEM((kv_heads, most, HD), BF16),
        pltpu.VMEM((kv_heads, most, 2 * HD), BF16),
        pltpu.VMEM((2, span, most), F32),
        pltpu.VMEM((2, span, most), BF16),
    ]
    if before is not None:
        operands.append(before)
        ins.append(VMEM)
        out, out_specs = (struct(*q.shape, dtype=BF16), out), (HBM, VMEM)
        scratch.append(pltpu.SemaphoreType.DMA)
    return call(
        functools.partial(attention_kernel, heads, groups, total),
        "attention",
        out,
        ins,
        out_specs,
        scratch,
        mib=16 + most * span * 12 // 2**20,
        after=after,
        held=held,
    )(*operands)


def per_device(
    xs, gate_z, b_in, c_in, log_decay, d_skip, norm_gain, queries, keys_new, values_new, kv_pool,
    state_pool, new_len, cached_blocks, kv_owner, kv_slot, state_owner, state_slot,
):
    total = lax.axis_size("batch")
    mp = lax.axis_size("mp")
    channels_all = xs.shape[2] * mp
    entries, pieces = kv_slot.shape[1], state_slot.shape[1]
    xs, gate_z, b_in, c_in, decay = xs[0], gate_z[0], b_in[0], c_in[0], log_decay[0]
    queries, keys_new, values_new = queries[0], keys_new[0], values_new[0]
    new_len, cached_blocks = new_len.reshape(1, 1), cached_blocks.reshape(1, 1)

    beside = [(0, 1), (1, 0), (2, 3), (3, 2)]
    across = [(0, 2), (1, 3)]

    lists = jnp.concatenate(
        [kv_owner.reshape(-1), kv_slot.reshape(-1), state_owner.reshape(-1), state_slot.reshape(-1)]
    )
    lists = lists + zeros(lists.shape[0])
    fresh = laid_together([keys_new, values_new], (lists,))
    far = lax.ppermute(fresh, "seq", across)
    sent, end, through, running, running_t = end_state(new_len, decay.T, b_in, xs, (fresh,))
    met = lax.ppermute(sent, "seq", beside)

    scan_operands = (new_len, running, running_t, b_in, c_in, xs, d_skip[None])
    kv_received, st_received, kept = [], [], None
    for shift in range(1, total):
        there = [(i, (i + shift) % total) for i in range(total)]
        back = [(j, i) for i, j in there]
        asked = lax.ppermute(lists, "batch", there)
        found = look_up(
            asked, lists, entries, pieces, kv_pool, state_pool, kept is None, (sent,)
        )
        if kept is None:
            kept = found[2:]
        kv_received.append(lax.ppermute(found[0], "batch", back))
        st_received.append(lax.ppermute(found[1], "batch", back))
    if total > 2:
        kv_received = jnp.concatenate(kv_received, axis=0)
        st_received = jnp.concatenate(st_received, axis=0)
    else:
        kv_received, st_received = kv_received[0], st_received[0]
    kv_kept, st_kept = kept

    sent = middle_state(met, end, through, (kv_kept,))
    middle = lax.ppermute(sent, "seq", across)
    quarter = xs.shape[1] // 4
    local = [local_scan(0, 2 * quarter, scan_operands, (sent,))]
    both = laid_together([fresh, far], (local[0],))
    near = lax.ppermute(both, "seq", beside)
    local.append(local_scan(2 * quarter, quarter, scan_operands, (both,)))
    q_heads = queries.shape[1] // HD
    later = q_heads // 4

    def attend(heads, before, after, held):
        return attention(
            heads, total, new_len, cached_blocks, lists, queries, keys_new, values_new, far, near,
            kv_kept, kv_received, before, after, held,
        )

    early = attend(tuple(range(q_heads - later)), None, (local[1],), (gate_z,))
    held = laid_together([middle], (early,))
    swapped = lax.ppermute(held, "seq", beside)[0]
    local.append(local_scan(3 * quarter, quarter, scan_operands, (held,)))
    cached = cached_state(lists, 2 * entries, total, st_kept, st_received, (local[2],))
    gated, squares = gate_output(running, c_in, gate_z, cached, met, middle, swapped, local)
    sums = [squares]
    for shift in range(1, mp):
        sums.append(lax.ppermute(squares, "mp", [(i, (i + shift) % mp) for i in range(mp)]))
    attended, late = attend(tuple(range(q_heads - later, q_heads)), early, (squares,), ())
    ssm_out, attended = norm_output(
        new_len, gated, norm_gain[None], sums, channels_all, late, attended
    )
    return (ssm_out[None], attended[None])


def solution(mesh):
    in_specs = (
        P("batch", "seq", "mp"),
        P("batch", "seq", "mp"),
        P("batch", "seq", None),
        P("batch", "seq", None),
        P("batch", "seq", "mp"),
        P("mp"),
        P("mp"),
        P("batch", "seq", "mp"),
        P("batch", "seq", "mp"),
        P("batch", "seq", "mp"),
        P("batch", None, None, "mp"),
        P("batch", "mp", None, None),
        P("batch"),
        P("batch"),
        P("batch", None, None),
        P("batch", None),
        P("batch", None, None),
        P("batch", None),
    )
    out_specs = (P("batch", "seq", "mp"), P("batch", "seq", "mp"))
    return jax.shard_map(
        per_device, mesh=mesh, in_specs=in_specs, out_specs=out_specs, check_vma=False
    )
```

```python
import functools

import jax
import jax.numpy as jnp
from jax import lax
from jax.experimental import pallas as pl
from jax.experimental.pallas import tpu as pltpu
from jax.sharding import PartitionSpec as P

P_SIZE = 64
HD = 128
CAP = 3
BQ = 128
NORM_PARTS = 8
EPSILON = 1e-05
NEGATIVE = -1e30
LOG2E = 1.4426950408889634
HIGHEST = lax.Precision.HIGHEST
F32 = jnp.float32
BF16 = jnp.bfloat16

SMEM = pl.BlockSpec(memory_space=pltpu.SMEM)
ANY = pl.BlockSpec(memory_space=pl.ANY)
VMEM = pl.BlockSpec(memory_space=pltpu.VMEM)
HBM = pl.BlockSpec(memory_space=pltpu.HBM)


def call(kernel, name, out, ins, outs, scratch=(), mib=16, after=(), held=(), aliases=None):
    count = len(ins)
    unread = (*after, *held)

    def body(*refs):
        kernel(*refs[:count], *refs[count + len(unread) :])

    run = pl.pallas_call(
        body,
        out_shape=out,
        in_specs=list(ins) + [ANY] * len(after) + [VMEM] * len(held),
        out_specs=outs,
        scratch_shapes=list(scratch),
        input_output_aliases=aliases or {},
        compiler_params=pltpu.CompilerParams(vmem_limit_bytes=mib * 1024 * 1024),
        cost_estimate=pl.CostEstimate(flops=10**10, bytes_accessed=10**7, transcendentals=0),
        name=name,
    )
    return lambda *operands: run(*operands, *unread)


def struct(*shape, dtype=F32):
    return jax.ShapeDtypeStruct(shape, dtype)


def mm(a, b):
    return jnp.dot(a, b, preferred_element_type=F32)


def mm_nt(a, b):
    return lax.dot_general(a, b, (((1,), (1,)), ((), ())), preferred_element_type=F32)


def split(value, terms, axis=1):
    parts = []
    rest = value
    for term in range(terms):
        part = rest.astype(BF16)
        parts.append(part)
        if term + 1 < terms:
            rest = rest - part.astype(F32)
    return jnp.concatenate(parts, axis=axis)


def spread_matrix(heads, terms, first_head, width):
    row = lax.broadcasted_iota(jnp.int32, (heads, width), 0)
    lane = lax.broadcasted_iota(jnp.int32, (heads, width), 1)
    one = jnp.where(row == (lane >> 6) + first_head, 1.0, 0.0).astype(BF16)
    return jnp.concatenate([one] * terms, axis=0)


def valid_rows(new_len, span):
    position = lax.axis_index("seq") * span + lax.broadcasted_iota(jnp.int32, (span, 1), 0)
    return position < new_len[...]


def slots_of(lists, base, count, owner):
    found, seen = [jnp.int32(0)] * CAP, jnp.int32(0)
    for e in range(count):
        match = lists[base + e] == owner
        slot = lists[base + count + e]
        found = [jnp.where(match & (seen == k), slot, at) for k, at in enumerate(found)]
        seen = seen + match.astype(jnp.int32)
    return found


def place_of(lists, base, count, e, total):
    owner = lists[base + e]
    shift = owner - lax.axis_index("batch")
    shift = jnp.where(shift < 0, shift + total, shift)
    rank = lax.fori_loop(
        0, e, lambda f, n: n + (lists[base + f] == owner).astype(jnp.int32), jnp.int32(0)
    )
    mine = shift == 0
    taken = (shift - 1) * CAP + jnp.minimum(rank, CAP - 1)
    return mine, jnp.where(mine, 0, taken)


def lookup_kernel(entries, pieces, asked, lists, kv_pool, st_pool, *outs):
    me = lax.axis_index("batch")
    for k, slot in enumerate(slots_of(asked, 0, entries, me)):
        outs[0][k] = kv_pool[slot]
    for k, slot in enumerate(slots_of(asked, 2 * entries, pieces, me)):
        outs[1][k] = st_pool[slot]
    if len(outs) > 2:
        for e in range(entries):
            outs[2][e] = kv_pool[lists[entries + e]]
        for e in range(pieces):
            outs[3][e] = st_pool[lists[2 * entries + pieces + e]]


def look_up(asked, lists, entries, pieces, kv_pool, st_pool, own, after):
    kv, st = kv_pool.shape[1:], st_pool.shape[1:]
    out = [struct(CAP, *kv, dtype=BF16), struct(CAP, *st, dtype=BF16)]
    if own:
        out += [struct(entries, *kv, dtype=BF16), struct(pieces, *st, dtype=BF16)]
    return call(
        functools.partial(lookup_kernel, entries, pieces),
        "look_up",
        tuple(out),
        [SMEM, SMEM, VMEM, VMEM],
        (VMEM,) * len(out),
        after=after,
    )(asked, lists, kv_pool, st_pool)


def zeros_kernel(out):
    out[...] = jnp.zeros_like(out)


def zeros(count):
    return call(zeros_kernel, "zeros", struct(1, count, dtype=jnp.int32), [], VMEM)()[0]


def laid_kernel(count, *refs):
    out = refs[count]
    begin = 0
    for ref in refs[:count]:
        if len(ref.shape) == 2:
            out[begin] = ref[...]
            begin += 1
        else:
            out[begin : begin + ref.shape[0]] = ref[...]
            begin += ref.shape[0]


def laid_together(parts, after):
    rows = sum(part.shape[0] if part.ndim == 3 else 1 for part in parts)
    return call(
        functools.partial(laid_kernel, len(parts)),
        "laid_together",
        struct(rows, *parts[0].shape[-2:], dtype=BF16),
        [VMEM] * len(parts),
        VMEM,
        after=after,
    )(*parts)


def end_state_kernel(new_len, decay_t, b_in, xs, sent, end, through, running, running_t):
    span, channels = xs.shape
    heads = decay_t.shape[0]
    n = b_in.shape[1]
    lane = lax.axis_index("seq") * span + lax.broadcasted_iota(jnp.int32, (1, span), 1)
    dec = jnp.where(lane < new_len[...], decay_t[...], 0.0)
    row = lax.broadcasted_iota(jnp.int32, (span, span), 0)
    col = lax.broadcasted_iota(jnp.int32, (span, span), 1)
    upper = jnp.where(row <= col, 1.0, 0.0).astype(BF16)
    r3 = mm(split(dec, 3, 0), upper)
    r_t = r3[:heads] + r3[heads : 2 * heads] + r3[2 * heads :]
    running_t[...] = r_t
    r = r_t.T
    running[...] = r
    last = r[span - 1 :, :]
    remain = split(jnp.exp(last - r), 2)
    lasting = split(jnp.broadcast_to(jnp.exp(last), (8, heads)), 3)
    b_t = jnp.where(valid_rows(new_len, span), b_in[...].astype(F32), 0.0).T.astype(BF16)
    width = min(512, channels)
    for begin in range(0, channels, width):
        lanes = slice(begin, begin + width)
        spread = spread_matrix(heads, 3, begin // P_SIZE, width)
        factor = mm(remain, spread[: 2 * heads])
        weighted = (xs[:, lanes].astype(F32) * factor).astype(BF16)
        state = mm(b_t, weighted)
        end[:, lanes] = state
        sent[:n, lanes] = state.astype(BF16)
        whole = mm(lasting, spread)
        through[:, lanes] = whole
        sent[n:, lanes] = jnp.concatenate(
            [split(whole[:1], 3, 0), jnp.zeros((13, width), BF16)], axis=0
        )


def end_state(new_len, decay_t, b_in, xs, after):
    span, channels = xs.shape
    heads = decay_t.shape[0]
    n = b_in.shape[1]
    return call(
        end_state_kernel,
        "end_state",
        (
            struct(n + 16, channels, dtype=BF16),
            struct(n, channels),
            struct(8, channels),
            struct(span, heads),
            struct(heads, span),
        ),
        [VMEM] * 4,
        (VMEM,) * 5,
        after=after,
    )(new_len, decay_t, b_in, xs)


def local_scan_kernel(
    begin, new_len, running, running_t, b_in, c_in, xs, d_skip, out, cols, inter, skips, into, outof
):
    span, channels = xs.shape
    heads = running.shape[1]
    here_channels = out.shape[1]
    width = min(512, here_channels)
    group = width // P_SIZE
    blocks = span // BQ
    r = running[...]
    for g in range(here_channels // width):
        first = begin // P_SIZE + g * group
        cols[g] = r[:, first : first + group]
    for i in range(1, blocks):
        edge = r[i * BQ - 1 : i * BQ, :]
        into[i - 1, : i * BQ] = split(jnp.exp(edge - r[: i * BQ]), 2)
        outof[i - 1] = split(jnp.exp(r[i * BQ : (i + 1) * BQ] - edge), 2)
    b = jnp.where(valid_rows(new_len, span), b_in[...].astype(F32), 0.0).astype(BF16)
    inter[...] = mm_nt(c_in[...], b)
    spread = spread_matrix(heads, 3, begin // P_SIZE, here_channels)
    skips[...] = mm(split(jnp.broadcast_to(d_skip[...], (8, heads)), 3), spread)
    lower = lax.broadcasted_iota(jnp.int32, (BQ, BQ), 0) >= lax.broadcasted_iota(
        jnp.int32, (BQ, BQ), 1
    )
    left = lax.broadcasted_iota(jnp.int32, (span, 2 * P_SIZE), 1) < P_SIZE

    def heads_of(step, unused):
        col = cols[step]
        first = begin // P_SIZE + step * group
        row = running_t[pl.ds(pl.multiple_of(first, group), group), :]
        x_group = xs[:, pl.ds(pl.multiple_of(begin + step * width, width), width)]
        spread = spread_matrix(heads, 2, first, width)
        earlier = [None]
        for i in range(1, blocks):
            factor = mm(into[i - 1, : i * BQ], spread)
            weighted = (x_group[: i * BQ].astype(F32) * factor).astype(BF16)
            product = mm(inter[i * BQ : (i + 1) * BQ, : i * BQ].astype(BF16), weighted)
            earlier.append(product * mm(outof[i - 1], spread))
        for pair in range(group // 2):
            at = slice(pair * 2 * P_SIZE, (pair + 1) * 2 * P_SIZE)
            offset = step * width + pair * 2 * P_SIZE
            lanes = pl.ds(pl.multiple_of(offset, 2 * P_SIZE), 2 * P_SIZE)
            x_pair = x_group[:, at]
            zero = jnp.zeros_like(x_pair)
            sides = (jnp.where(left, x_pair, zero), jnp.where(left, zero, x_pair))
            for i in range(blocks):
                here = slice(i * BQ, (i + 1) * BQ)
                lhs, rhs = [], []
                for side in range(2):
                    h = pair * 2 + side
                    gap = jnp.broadcast_to(col[here, h : h + 1], (BQ, BQ)) - row[h : h + 1, here]
                    gap = jnp.where(lower, gap, NEGATIVE)
                    lhs.append((jnp.exp(gap) * inter[here, here]).astype(BF16))
                    rhs.append(sides[side][here])
                y = mm(jnp.concatenate(lhs, axis=1), jnp.concatenate(rhs, axis=0))
                y = y + skips[:1, lanes] * x_pair[here].astype(F32)
                out[here, lanes] = y if i == 0 else y + earlier[i][:, at]
        return unused

    lax.fori_loop(0, here_channels // width, heads_of, 0, unroll=True)


def local_scan(begin, size, operands, after):
    span = operands[-2].shape[0]
    heads = operands[1].shape[1]
    width = min(512, size)
    blocks = span // BQ
    return call(
        functools.partial(local_scan_kernel, begin),
        "local_scan",
        struct(span, size),
        [VMEM] * 7,
        VMEM,
        [
            pltpu.VMEM((size // width, span, width // P_SIZE), F32),
            pltpu.VMEM((span, span), F32),
            pltpu.VMEM((8, size), F32),
            pltpu.VMEM((blocks - 1, span, 2 * heads), BF16),
            pltpu.VMEM((blocks - 1, BQ, 2 * heads), BF16),
        ],
        after=after,
    )(*operands)


def kept_factors(sent, n, lanes=slice(None)):
    return jnp.sum(sent[n : n + 16, lanes].astype(F32), axis=0, keepdims=True)


def middle_kernel(received, end, through, sent):
    seq = lax.axis_index("seq")
    n, channels = end.shape
    half = channels // 2

    def combine(lanes, early_e, early_t, late_e, late_t):
        sent[:n, :] = (late_t * early_e[:n, lanes].astype(F32) + late_e[:n, lanes]).astype(BF16)
        rest = jnp.zeros((13, half), BF16)
        sent[n:, :] = jnp.concatenate([split(late_t * early_t, 3, 0), rest], axis=0)

    @pl.when(seq == 0)
    def _():
        lanes = slice(0, half)
        combine(lanes, end, through[:1, lanes], received, kept_factors(received, n, lanes))

    @pl.when(seq == 1)
    def _():
        lanes = slice(half, channels)
        combine(lanes, received, kept_factors(received, n, lanes), end, through[:1, lanes])


def middle_state(received, end, through, after):
    return call(
        middle_kernel,
        "middle_state",
        struct(received.shape[0], received.shape[1] // 2, dtype=BF16),
        [VMEM] * 3,
        VMEM,
        after=after,
    )(received, end, through)


def cached_kernel(base, total, lists, kept_in, taken_in, out):
    pieces, heads = kept_in.shape[:2]
    places = [place_of(lists, base, pieces, j, total) for j in range(pieces)]
    for h in range(0, heads, 2):
        parts = [
            jnp.where(mine, kept_in[j, h + k], taken_in[taken, h + k])
            for k in range(2)
            for j, (mine, taken) in enumerate(places)
        ]
        lanes = slice(h * P_SIZE, (h + 2) * P_SIZE)
        out[:, lanes] = jnp.concatenate(parts, axis=0).astype(F32).T.astype(BF16)


def cached_state(lists, base, total, kept, received, after):
    pieces, heads, rows, n = kept.shape
    channels = heads * pieces * rows
    if rows % 16 == 0:
        return call(
            functools.partial(cached_kernel, base, total),
            "cached_state",
            struct(n, channels, dtype=BF16),
            [SMEM, VMEM, VMEM],
            VMEM,
            after=after,
        )(lists, kept, received)
    owners = lists[base : base + pieces]
    shift = (owners - lax.axis_index("batch")) % total
    order = jnp.arange(pieces)
    same = (owners[:, None] == owners[None, :]) & (order[:, None] > order[None, :])
    rank = jnp.minimum(jnp.sum(same.astype(jnp.int32), axis=1), CAP - 1)
    mine = shift == 0
    taken = received[jnp.where(mine, 0, (shift - 1) * CAP + rank)]
    found = jnp.where(mine[:, None, None, None], kept, taken)
    return jnp.transpose(found, (3, 1, 0, 2)).reshape(n, channels)


def gate_kernel(count, running, c_in, gate, cached, met, middle, swapped, *rest):
    locals_in, (gated, squares) = rest[:count], rest[count:]
    span, channels = gate.shape
    heads = running.shape[1]
    n = c_in.shape[1]
    width = 256
    seq = lax.axis_index("seq")
    far, odd = seq >= 2, seq % 2 == 1

    def entering(begin):
        state = cached[:, begin : begin + width].astype(F32)
        side, at = divmod(begin, channels // 2)
        lanes = slice(at, at + width)
        part = jnp.where(odd == (side == 1), middle[:, lanes], swapped[:, lanes])
        kept = jnp.where(far, kept_factors(part, n), 1.0)
        state = kept * state + jnp.where(far, part[:n].astype(F32), 0.0)
        lanes = slice(begin, begin + width)
        kept = jnp.where(odd, kept_factors(met, n, lanes), 1.0)
        state = kept * state + jnp.where(odd, met[:n, lanes].astype(F32), 0.0)
        return state.astype(BF16)

    factors = split(jnp.exp(running[...]), 2)
    c = c_in[...]
    total = jnp.zeros((span, 128), F32)
    begin = 0
    for local in locals_in:
        for at in range(0, local.shape[1], width):
            lanes = slice(begin + at, begin + at + width)
            factor = mm(factors, spread_matrix(heads, 2, (begin + at) // P_SIZE, width))
            carried = mm(c, entering(begin + at))
            z = gate[:, lanes].astype(F32)
            value = (local[:, at : at + width] + factor * carried) * (z / (1.0 + jnp.exp(-z)))
            gated[:, lanes] = value.astype(BF16)
            square = value * value
            for k in range(width // 128):
                total = total + square[:, k * 128 : (k + 1) * 128]
        begin += local.shape[1]
    ones = jnp.ones((8, 128), F32)
    squares[...] = lax.dot_general(
        ones, total, (((1,), (1,)), ((), ())), precision=HIGHEST, preferred_element_type=F32
    )


def gate_output(running, c_in, gate, cached, met, middle, swapped, local):
    span, channels = gate.shape
    return call(
        functools.partial(gate_kernel, len(local)),
        "gate",
        (struct(span, channels, dtype=BF16), struct(8, span)),
        [VMEM] * (7 + len(local)),
        (VMEM, VMEM),
    )(running, c_in, gate, cached, met, middle, swapped, *local)


def norm_kernel(all_channels, count, new_len, gated, gain, late, *rest):
    sums, (out, attended, staged, sems) = rest[:count], rest[count + 1 :]
    span, channels = gated.shape
    rows_each = span // NORM_PARTS
    begin = attended.shape[1] - late.shape[1]
    copies = [
        pltpu.make_async_copy(late, attended.at[:, pl.ds(begin, late.shape[1])], sems.at[0])
    ]
    copies[0].start()
    total = sums[0][...]
    for part in sums[1:]:
        total = total + part[...]
    scale = lax.rsqrt(total / all_channels + EPSILON).T[:, :1]
    scale = jnp.where(valid_rows(new_len, span), scale, 0.0)
    for begin in range(0, span, rows_each):
        rows = slice(begin, begin + rows_each)
        staged[rows] = (gated[rows].astype(F32) * scale[rows] * gain[...]).astype(BF16)
        at = pl.ds(begin, rows_each)
        copies.append(pltpu.make_async_copy(staged.at[at], out.at[at], sems.at[len(copies)]))
        copies[-1].start()
    for copy in copies:
        copy.wait()


def norm_output(new_len, gated, gain, sums, all_channels, late, attended):
    span, channels = gated.shape
    copies = 1 + NORM_PARTS
    return call(
        functools.partial(norm_kernel, all_channels, len(sums)),
        "norm",
        (struct(span, channels, dtype=BF16), struct(*attended.shape, dtype=BF16)),
        [VMEM] * (4 + len(sums)) + [HBM],
        (HBM, HBM),
        [pltpu.VMEM((span, channels), BF16), pltpu.SemaphoreType.DMA((copies,))],
        aliases={4 + len(sums): 1},
    )(new_len, gated, gain, late, *sums, attended)


def attention_kernel(
    heads, groups, total, new_len, cached, lists, q, own_k, own_v, far, near, kept, received, *rest
):
    if len(rest) > 5:
        before, out, staged, keys, values, scores, weights, sem = rest
        done = before.shape[1]
        copy = pltpu.make_async_copy(before, out.at[:, pl.ds(0, done)], sem)
        copy.start()
    else:
        copy = None
        staged, keys, values, scores, weights = rest
    span = own_k.shape[0]
    entries, rows_each = kept.shape[0], kept.shape[2]
    kv_heads = sorted({head // groups for head in heads})
    seq = lax.axis_index("seq")
    cached_len = entries * rows_each
    few = 2 * span + cached_len
    factor = HD ** (-0.5) * LOG2E

    def put(begin, key_rows, value_rows):
        rows = slice(begin, begin + key_rows.shape[0])
        for h, kv_head in enumerate(kv_heads):
            lanes = slice(kv_head * HD, (kv_head + 1) * HD)
            keys[h, rows] = key_rows[:, lanes]
            values[h, rows, :HD] = value_rows[:, lanes]
            values[h, rows, HD:] = jnp.ones_like(value_rows[:, lanes])

    put(0, own_k[...], own_v[...])
    put(span + cached_len, near[0], near[1])
    for e in range(entries):
        mine, taken = place_of(lists, 0, entries, e, total)
        record = [jnp.where(mine, kept[e, k], received[taken, k]) for k in (0, 1)]
        put(span + e * rows_each, *record)
    key = lax.broadcasted_iota(jnp.int32, (1, few - span), 1)
    open_keys = (key < cached[...] * rows_each) | ((key >= cached_len) & (seq % 2 == 1))
    bias = jnp.where(open_keys, 0.0, NEGATIVE)
    valid = valid_rows(new_len, span)

    def attend(count):
        for k, head in enumerate(heads):
            slot, kv_head = k % 2, kv_heads.index(head // groups)
            scores[slot, :, :count] = mm_nt(q[:, head * HD : (head + 1) * HD], keys[kv_head, :count])
            for begin in range(0, span, BQ):
                rows = slice(begin, begin + BQ)
                s = scores[slot, rows, :count]
                at = lax.broadcasted_iota(jnp.int32, (BQ, span), 0) + begin
                past = at >= lax.broadcasted_iota(jnp.int32, (BQ, span), 1)
                parts = [jnp.where(past, s[:, :span], NEGATIVE), s[:, span:few] + bias]
                if count > few:
                    parts.append(s[:, few:])
                s = jnp.concatenate(parts, axis=1)
                high = jnp.max(s, axis=1, keepdims=True)
                weights[slot, rows, :count] = jnp.exp2(s * factor - high * factor).astype(BF16)
            summed = mm(weights[slot, :, :count], values[kv_head, :count])
            ratio = summed[:, :HD] / summed[:, HD:]
            staged[:, k * HD : (k + 1) * HD] = jnp.where(valid, ratio, 0.0).astype(BF16)

    @pl.when(seq < 2)
    def _():
        attend(few)

    @pl.when(seq >= 2)
    def _():
        put(few, far[0], far[1])
        put(few + span, near[2], near[3])
        attend(few + 2 * span)

    if copy is not None:
        copy.wait()


def attention(
    heads, total, new_len, cached, lists, q, keys, values, far, near, kept, received, before, after,
    held,
):
    span = q.shape[0]
    groups = q.shape[1] // keys.shape[1]
    kv_heads = len({head // groups for head in heads})
    most = 4 * span + kept.shape[0] * kept.shape[2]
    operands = [new_len, cached, lists, q, keys, values, far, near, kept, received]
    ins = [VMEM, VMEM, SMEM] + [VMEM] * 7
    out, out_specs = struct(span, len(heads) * HD, dtype=BF16), VMEM
    scratch = [
        pltpu.VMEM((kv_heads, most, HD), BF16),
        pltpu.VMEM((kv_heads, most, 2 * HD), BF16),
        pltpu.VMEM((2, span, most), F32),
        pltpu.VMEM((2, span, most), BF16),
    ]
    if before is not None:
        operands.append(before)
        ins.append(VMEM)
        out, out_specs = (struct(*q.shape, dtype=BF16), out), (HBM, VMEM)
        scratch.append(pltpu.SemaphoreType.DMA)
    return call(
        functools.partial(attention_kernel, heads, groups, total),
        "attention",
        out,
        ins,
        out_specs,
        scratch,
        mib=16 + most * span * 12 // 2**20,
        after=after,
        held=held,
    )(*operands)


def per_device(
    xs, gate_z, b_in, c_in, log_decay, d_skip, norm_gain, queries, keys_new, values_new, kv_pool,
    state_pool, new_len, cached_blocks, kv_owner, kv_slot, state_owner, state_slot,
):
    total = lax.axis_size("batch")
    mp = lax.axis_size("mp")
    channels_all = xs.shape[2] * mp
    entries, pieces = kv_slot.shape[1], state_slot.shape[1]
    xs, gate_z, b_in, c_in, decay = xs[0], gate_z[0], b_in[0], c_in[0], log_decay[0]
    queries, keys_new, values_new = queries[0], keys_new[0], values_new[0]
    new_len, cached_blocks = new_len.reshape(1, 1), cached_blocks.reshape(1, 1)

    beside = [(0, 1), (1, 0), (2, 3), (3, 2)]
    across = [(0, 2), (1, 3)]

    lists = jnp.concatenate(
        [kv_owner.reshape(-1), kv_slot.reshape(-1), state_owner.reshape(-1), state_slot.reshape(-1)]
    )
    lists = lists + zeros(lists.shape[0])
    fresh = laid_together([keys_new, values_new], (lists,))
    far = lax.ppermute(fresh, "seq", across)
    sent, end, through, running, running_t = end_state(new_len, decay.T, b_in, xs, (fresh,))
    met = lax.ppermute(sent, "seq", beside)

    scan_operands = (new_len, running, running_t, b_in, c_in, xs, d_skip[None])
    kv_received, st_received, kept = [], [], None
    for shift in range(1, total):
        there = [(i, (i + shift) % total) for i in range(total)]
        back = [(j, i) for i, j in there]
        asked = lax.ppermute(lists, "batch", there)
        found = look_up(
            asked, lists, entries, pieces, kv_pool, state_pool, kept is None, (sent,)
        )
        if kept is None:
            kept = found[2:]
        kv_received.append(lax.ppermute(found[0], "batch", back))
        st_received.append(lax.ppermute(found[1], "batch", back))
    if total > 2:
        kv_received = jnp.concatenate(kv_received, axis=0)
        st_received = jnp.concatenate(st_received, axis=0)
    else:
        kv_received, st_received = kv_received[0], st_received[0]
    kv_kept, st_kept = kept

    sent = middle_state(met, end, through, (kv_kept,))
    middle = lax.ppermute(sent, "seq", across)
    quarter = xs.shape[1] // 4
    local = [local_scan(0, 2 * quarter, scan_operands, (sent,))]
    both = laid_together([fresh, far], (local[0],))
    near = lax.ppermute(both, "seq", beside)
    local.append(local_scan(2 * quarter, quarter, scan_operands, (both,)))
    q_heads = queries.shape[1] // HD
    later = q_heads // 4

    def attend(heads, before, after, held):
        return attention(
            heads, total, new_len, cached_blocks, lists, queries, keys_new, values_new, far, near,
            kv_kept, kv_received, before, after, held,
        )

    early = attend(tuple(range(q_heads - later)), None, (local[1],), (gate_z,))
    held = laid_together([middle], (early,))
    swapped = lax.ppermute(held, "seq", beside)[0]
    local.append(local_scan(3 * quarter, quarter, scan_operands, (held,)))
    cached = cached_state(lists, 2 * entries, total, st_kept, st_received, (local[2],))
    gated, squares = gate_output(running, c_in, gate_z, cached, met, middle, swapped, local)
    sums = [squares]
    for shift in range(1, mp):
        pairs = [(i, i ^ shift if mp & (mp - 1) == 0 else (i + shift) % mp) for i in range(mp)]
        sums.append(lax.ppermute(squares, "mp", pairs))
    attended, late = attend(tuple(range(q_heads - later, q_heads)), early, (squares,), ())
    ssm_out, attended = norm_output(
        new_len, gated, norm_gain[None], sums, channels_all, late, attended
    )
    return (ssm_out[None], attended[None])


def solution(mesh):
    in_specs = (
        P("batch", "seq", "mp"),
        P("batch", "seq", "mp"),
        P("batch", "seq", None),
        P("batch", "seq", None),
        P("batch", "seq", "mp"),
        P("mp"),
        P("mp"),
        P("batch", "seq", "mp"),
        P("batch", "seq", "mp"),
        P("batch", "seq", "mp"),
        P("batch", None, None, "mp"),
        P("batch", "mp", None, None),
        P("batch"),
        P("batch"),
        P("batch", None, None),
        P("batch", None),
        P("batch", None, None),
        P("batch", None),
    )
    out_specs = (P("batch", "seq", "mp"), P("batch", "seq", "mp"))
    return jax.shard_map(
        per_device, mesh=mesh, in_specs=in_specs, out_specs=out_specs, check_vma=False
    )
```
